512 devices in a mesh: seq: 64 (over x, z, core), kvh: 8 (over y).
Axes of the slice: x: 4, y: 8, z: 8, core: 2. Of those that a mesh axis runs over, the one named last changes fastest.
Arguments:
- queries: bfloat16 [128, 2, 64, 128], P('seq', None, 'kvh'), may hold values from -6 to 6
- new_keys: bfloat16 [128, 2, 8, 128], P('seq', None, 'kvh'), may hold values from -12 to 12
- new_values: bfloat16 [128, 2, 8, 128], P('seq', None, 'kvh'), may hold values from -6 to 6
- prefix_keys: bfloat16 [16384, 8, 128], P('seq', 'kvh'), may hold values from -12 to 12
- prefix_values: bfloat16 [16384, 8, 128], P('seq', 'kvh'), may hold values from -6 to 6
- prompt_keys: bfloat16 [32768, 8, 128], P('seq', 'kvh'), may hold values from -12 to 12
- prompt_values: bfloat16 [32768, 8, 128], P('seq', 'kvh'), may hold values from -6 to 6
- cache_keys: bfloat16 [128, 256, 8, 128], P('seq', None, 'kvh'), may hold values from -12 to 12
- cache_values: bfloat16 [128, 256, 8, 128], P('seq', None, 'kvh'), may hold values from -6 to 6
- group_prompt: int32 [16], replicated, may hold values from 0 to 15, each once
- prompt_len: int32 [16], replicated, may hold values from 256 to 2048, as said below
- cont_prompt: int32 [128], replicated, may hold values from 0 to 15, as said below
- cont_len: int32 [128], P('seq'), may hold values from 1 to 256, as said below
- out_weight: bfloat16 [8192, 5120], P('kvh', 'seq'), may hold values from -0.0625 to 0.0625
Outputs:
- output: float32 [128, 2, 5120], P('kvh', None, 'seq')
The draws below stay inside these ranges and needn't reach their ends.
Inputs may be any that keep to these rules, and one draw needn't show every extreme that they name: `cont_prompt`: every prompt has exactly 8 continuations. `prompt_len`: the longest prompt has exactly 2048 tokens and the shortest 2048 // 8. `cont_len`: some continuation uses all 256 cache rows and some only one.
All inputs are finite; a program needn't handle non-finite values.
Results may differ from the reference program's by a relative error of at most 0.0021.
The reference program's roundings to bfloat16 on the way (of `weights` and `attention`) count: a program that leaves them out, or rounds other values in their place, can miss the bound.
Values may be sent and summed in bfloat16 or wider, within the bound.
A program may use at most 192 MiB of HBM per device.

```python
import math
import jax
import jax.numpy as jnp
from jax import lax

D = 5120
H = 64
KVH = 8
HD = 128
NEW = 2
PROMPTS = 16
PRE_DEV = 256
PLEN_DEV = 512
GEN = 256
CONTS = 128
PREFIX = 16384
PLEN = 2048
N_SEQ = 64


def draw_queries(key, part):
    key = jax.random.fold_in(key, 11)
    values = jnp.clip(jax.random.normal(key, (CONTS, NEW, H, HD), jnp.float32), -6.0, 6.0)
    return values.astype(jnp.bfloat16)


def draw_prefix_keys(key, part):
    key = jax.random.fold_in(key, 13)
    values = jnp.clip(3.0 * jax.random.normal(key, (PREFIX, KVH, HD), jnp.float32), -12.0, 12.0)
    return values.astype(jnp.bfloat16)


def draw_prompt_len(key, part):
    key = jax.random.fold_in(key, 31)
    first_key, second_key = jax.random.split(key)
    values = jax.random.randint(first_key, (PROMPTS,), PLEN // 8, PLEN + 1)
    order = jax.random.permutation(second_key, PROMPTS)
    values = jnp.where(order == 0, PLEN, values)
    values = jnp.where(order == 1, PLEN // 8, values)
    return values.astype(jnp.int32)


def draw_cont_prompt(key, part):
    key = jax.random.fold_in(key, 21)
    order = jax.random.permutation(key, CONTS)
    return (order % PROMPTS).astype(jnp.int32)


def draw_cont_len(key, part):
    key = jax.random.fold_in(key, 41)
    first_key, second_key = jax.random.split(key)
    values = jax.random.randint(first_key, (CONTS,), 1, GEN + 1)
    order = jax.random.permutation(second_key, CONTS)
    values = jnp.where(order == 0, GEN, values)
    values = jnp.where(order == 1, 1, values)
    return values.astype(jnp.int32)


def shard_levels(rng, dims, shards, least, largest):
    level = 1.0
    for axis_at, shards_of in shards:
        steps = jax.random.uniform(jax.random.fold_in(jax.random.fold_in(rng, 6), axis_at), (shards_of,), jnp.float32, least / len(shards), largest / len(shards))
        level = level * jnp.repeat(jnp.exp(steps), dims[axis_at] // shards_of).reshape((-1,) + (1,) * (len(dims) - 1 - axis_at))
    return level


def normal_values(own_key, dims, width, bound, pieces=(), kind=jnp.bfloat16):
    values = jax.random.normal(own_key, dims, jnp.float32) * width
    if len(pieces) > 0:
        values = shard_levels(own_key, dims, pieces, -0.22, 0.18) * values
    return jnp.clip(values, min=-bound, max=bound).astype(kind)


def setup_inputs(seed: int = 0) -> dict:
    key_of = jax.random.split(jax.random.key(seed), 15)
    return {
        "queries": draw_queries(jax.random.fold_in(key_of[14], 71), 0),
        "new_keys": normal_values(key_of[1], (CONTS, NEW, KVH, HD), 3.0, 12.0, ((0, 64), (2, 8))),
        "new_values": normal_values(key_of[2], (CONTS, NEW, KVH, HD), 1.0, 6.0, ((0, 64), (2, 8))),
        "prefix_keys": draw_prefix_keys(jax.random.fold_in(key_of[14], 71), 0),
        "prefix_values": normal_values(key_of[4], (PREFIX, KVH, HD), 1.0, 6.0, ((0, 64), (1, 8))),
        "prompt_keys": normal_values(key_of[5], (PLEN * PROMPTS, KVH, HD), 3.0, 12.0, ((0, 64), (1, 8))),
        "prompt_values": normal_values(key_of[6], (PLEN * PROMPTS, KVH, HD), 1.0, 6.0, ((0, 64), (1, 8))),
        "cache_keys": normal_values(key_of[7], (CONTS, GEN, KVH, HD), 3.0, 12.0, ((0, 64), (2, 8))),
        "cache_values": normal_values(key_of[8], (CONTS, GEN, KVH, HD), 1.0, 6.0, ((0, 64), (2, 8))),
        "group_prompt": jax.random.permutation(key_of[9], PROMPTS).astype(jnp.int32),
        "prompt_len": draw_prompt_len(jax.random.fold_in(key_of[14], 71), 0),
        "cont_prompt": draw_cont_prompt(jax.random.fold_in(key_of[14], 71), 0),
        "cont_len": draw_cont_len(jax.random.fold_in(key_of[14], 71), 0),
        "out_weight": normal_values(key_of[13], (H * HD, D), (H * HD) ** -0.5, 0.0625, ((0, 8), (1, 64))),
    }


NEG = -1e+30

def block_partial(query_rows, key_rows, value_rows, usable, scaling):
    scores = jnp.dot(query_rows, key_rows.T, preferred_element_type=jnp.float32) * scaling
    scores = jnp.where(usable, scores, NEG)
    maximum = lax.optimization_barrier(jnp.max(scores, axis=-1))
    weights = jnp.where(usable, jnp.exp(scores - maximum[..., None]), 0.0).astype(jnp.bfloat16)
    weights = lax.optimization_barrier(weights)
    totals = lax.optimization_barrier(jnp.sum(weights.astype(jnp.float32), axis=-1))
    weighted = jnp.dot(weights, value_rows, preferred_element_type=jnp.float32)
    return (maximum, totals, weighted)

def join_partials(former, latter):
    maximum = jnp.maximum(former[0], latter[0])
    former_scale = jnp.exp(former[0] - maximum)
    latter_scale = jnp.exp(latter[0] - maximum)
    return (maximum, former[1] * former_scale + latter[1] * latter_scale, former[2] * former_scale[..., None] + latter[2] * latter_scale[..., None])

def prompt_partial(all_queries, key_rows, value_rows, device, group_prompt, prompt_len, cont_prompt, group_span, per_prompt, scaling):
    cont_count, fresh_count, group_size, head_width = all_queries.shape
    prompts = group_prompt.shape[0]
    slot_ids = jnp.arange(prompts, dtype=jnp.int32)
    owned = jnp.sum(jnp.where(slot_ids == device // group_span, group_prompt, 0))
    length = jnp.sum(jnp.where(slot_ids == owned, prompt_len, 0))
    chosen = jnp.nonzero(cont_prompt == owned, size=per_prompt)[0].astype(jnp.int32)
    picked = all_queries[chosen].reshape(per_prompt * fresh_count * group_size, head_width)
    span_len = key_rows.shape[0]
    places = device % group_span * span_len + jnp.arange(span_len, dtype=jnp.int32)
    maximum, totals, weighted = block_partial(picked, key_rows, value_rows, (places < length)[None, :], scaling)
    shape3 = (per_prompt, fresh_count, group_size)
    full_max = jnp.full((cont_count, fresh_count, group_size), NEG, jnp.float32).at[chosen].set(maximum.reshape(shape3))
    full_tot = jnp.zeros((cont_count, fresh_count, group_size), jnp.float32).at[chosen].set(totals.reshape(shape3))
    full_wtd = jnp.zeros((cont_count, fresh_count, group_size, head_width), jnp.float32).at[chosen].set(weighted.reshape(shape3 + (head_width,)))
    return (full_max, full_tot, full_wtd)

def own_partial(local_queries, cache_k, cache_v, fresh_k, fresh_v, lengths, scaling):
    cont_count, fresh_count, group_size, head_width = local_queries.shape
    gen_len = cache_k.shape[1]
    query_float = local_queries.astype(jnp.float32)
    past = jnp.einsum('ctgd,cjd->ctgj', query_float, cache_k.astype(jnp.float32))
    recent = jnp.einsum('ctgd,cud->ctgu', query_float, fresh_k.astype(jnp.float32))
    scores = jnp.concatenate([past, recent], axis=3) * scaling
    usable_past = jnp.arange(gen_len, dtype=jnp.int32)[None, :] < lengths[:, None]
    usable_new = jnp.arange(fresh_count, dtype=jnp.int32)[None, :] <= jnp.arange(fresh_count, dtype=jnp.int32)[:, None]
    usable = jnp.concatenate([jnp.broadcast_to(usable_past[:, None, None, :], (cont_count, fresh_count, 1, gen_len)), jnp.broadcast_to(usable_new[None, :, None, :], (cont_count, fresh_count, 1, fresh_count))], axis=3)
    scores = jnp.where(usable, scores, NEG)
    maximum = lax.optimization_barrier(jnp.max(scores, axis=-1))
    weights = jnp.where(usable, jnp.exp(scores - maximum[..., None]), 0.0).astype(jnp.bfloat16)
    weights = lax.optimization_barrier(weights)
    weight_float = weights.astype(jnp.float32)
    totals = lax.optimization_barrier(jnp.sum(weight_float, axis=-1))
    weighted = jnp.einsum('ctgj,cjd->ctgd', weight_float[..., :gen_len], cache_v.astype(jnp.float32))
    weighted = weighted + jnp.einsum('ctgu,cud->ctgd', weight_float[..., gen_len:], fresh_v.astype(jnp.float32))
    return (maximum, totals, weighted)

def reference(queries, new_keys, new_values, prefix_keys, prefix_values, prompt_keys, prompt_values, cache_keys, cache_values, group_prompt, prompt_len, cont_prompt, cont_len, out_weight):
    group_size = H // KVH
    per_prompt = CONTS // PROMPTS
    group_span = N_SEQ // PROMPTS
    scaling = 1.0 / math.sqrt(HD)
    shaped = queries.reshape(CONTS, NEW, KVH, group_size, HD)

    def one_head(head_index):

        def select_head(source, axis_number):
            return lax.dynamic_index_in_dim(source, head_index, axis_number, keepdims=False)
        head_queries = select_head(shaped, 2)
        start_part = own_partial(head_queries, select_head(cache_keys, 2), select_head(cache_values, 2), select_head(new_keys, 2), select_head(new_values, 2), cont_len, scaling)
        prefix_k = select_head(prefix_keys, 1).reshape(N_SEQ, PRE_DEV, HD)
        prefix_v = select_head(prefix_values, 1).reshape(N_SEQ, PRE_DEV, HD)
        prompt_k = select_head(prompt_keys, 1).reshape(N_SEQ, PLEN_DEV, HD)
        prompt_v = select_head(prompt_values, 1).reshape(N_SEQ, PLEN_DEV, HD)
        query_rows = head_queries.reshape(CONTS * NEW * group_size, HD)
        every_key = jnp.ones((1, PRE_DEV), dtype=bool)
        shape3 = (CONTS, NEW, group_size)

        def visit(running, device):
            maximum, totals, weighted = block_partial(query_rows, prefix_k[device], prefix_v[device], every_key, scaling)
            prefix_part = (maximum.reshape(shape3), totals.reshape(shape3), weighted.reshape(shape3 + (HD,)))
            prompt_part = prompt_partial(head_queries, prompt_k[device], prompt_v[device], device, group_prompt, prompt_len, cont_prompt, group_span, per_prompt, scaling)
            return (join_partials(running, join_partials(prefix_part, prompt_part)), None)
        final, unused = lax.scan(visit, start_part, jnp.arange(N_SEQ, dtype=jnp.int32))
        return final[2] / final[1][..., None]
    heads_out = lax.map(one_head, jnp.arange(KVH, dtype=jnp.int32))
    attention = jnp.transpose(heads_out, (1, 2, 0, 3, 4)).reshape(CONTS * NEW, H * HD).astype(jnp.bfloat16)
    projected = jnp.dot(attention, out_weight, preferred_element_type=jnp.float32)
    return projected.reshape(CONTS, NEW, D)
```

```python
import functools
import math

import jax
import jax.numpy as jnp
from jax import lax
from jax.experimental import pallas as pl
from jax.experimental.pallas import tpu as pltpu
from jax.sharding import PartitionSpec as P

NEG = -1e30
MESH = pl.DeviceIdType.MESH
F32, BF16 = jnp.float32, jnp.bfloat16
NX, NZ, NC, NY = 4, 8, 2, 8
CHIPS = NX * NZ
ROWS = 32
HD = 128
GROUP = 8
SCALING = 1.0 / math.sqrt(HD)


def dot(a, b):
    return jnp.dot(a, b, preferred_element_type=F32)


def dot_nt(a, b):
    return lax.dot_general(a, b, (((1,), (1,)), ((), ())), preferred_element_type=F32)


def iota(shape, axis):
    return lax.broadcasted_iota(jnp.int32, shape, axis)


def loop(low, high, step):
    def run(k, carry):
        step(k)
        return carry

    lax.fori_loop(low, high, run, 0)


def remote(src, dst, send_sem, recv_sem, chip, y, core):
    return pltpu.make_async_remote_copy(
        src_ref=src,
        dst_ref=dst,
        send_sem=send_sem,
        recv_sem=recv_sem,
        device_id={"seq": chip * 2 + core, "kvh": y},
        device_id_type=MESH,
    )


def with_ones(values):
    flipped = jnp.transpose(values.astype(F32))
    return jnp.concatenate([flipped, jnp.ones((16, values.shape[0]), F32)], axis=0).astype(BF16)


def kernel(
    q_in,
    pk_in,
    pv_in,
    sk_in,
    sv_in,
    ck_in,
    cv_in,
    w_in,
    nk_ref,
    nv_ref,
    cont_prompt_ref,
    group_prompt_ref,
    prompt_len_ref,
    cont_len_ref,
    out_ref,
    q_all,
    pk,
    pv,
    sk,
    sv,
    ck,
    cv,
    wt,
    pvt,
    svt,
    member,
    x_send,
    x_recv,
    z_send,
    z_recv,
    att,
    att_f32,
    flat,
    y_send,
    y_recv,
    own_sem,
    swap_ss,
    swap_rs,
    q_ss,
    q_rs,
    x_ss,
    x_rs,
    z_ss,
    z_rs,
    a_ss,
    a_rs,
    y_ss,
    y_rs,
):
    seq = lax.axis_index("seq")
    y = lax.axis_index("kvh")
    chip, c = seq // 2, seq % 2
    x, z = chip // NZ, chip % NZ
    other = 1 - c
    yc = y * 2 + c

    barrier = pltpu.get_barrier_semaphore()

    def greet_plane(k):
        pl.semaphore_signal(
            barrier,
            inc=1,
            device_id={"seq": lax.rem(chip + k, CHIPS) * 2 + c, "kvh": y},
            device_id_type=MESH,
        )

    def greet_column(k):
        to = lax.rem(yc + k, 16)
        pl.semaphore_signal(
            barrier, inc=1, device_id={"seq": chip * 2 + to % 2, "kvh": to // 2}, device_id_type=MESH
        )

    loop(1, CHIPS, greet_plane)
    loop(1, 16, greet_column)

    local = [
        pltpu.make_async_copy(src, dst, own_sem.at[n])
        for n, (src, dst) in enumerate(
            [
                (q_in, q_all.at[chip]),
                (ck_in, ck),
                (cv_in, cv),
                (pk_in, pk.at[c]),
                (pv_in, pv.at[c]),
                (sk_in, sk.at[c]),
                (sv_in, sv.at[c]),
                (w_in, wt.at[c, pl.ds(0, 80)]),
            ]
        )
    ]
    for copy in local:
        copy.start()
    wt[:, 80:, :] = jnp.zeros((2, 48, wt.shape[2]), BF16)
    for copy in local[:3]:
        copy.wait()

    q_own = q_all[chip]
    first = iota((ROWS, 1), 0) < 16
    past0 = dot_nt(q_own, ck[0]) * SCALING
    past1 = dot_nt(q_own, ck[1]) * SCALING
    lengths = jnp.where(first, cont_len_ref[0], cont_len_ref[1])
    past = jnp.where(iota(past0.shape, 1) < lengths, jnp.where(first, past0, past1), NEG)
    fresh_pad = jnp.zeros((12, HD), F32)
    nk = jnp.concatenate([nk_ref[0].astype(F32), nk_ref[1].astype(F32), fresh_pad], axis=0).astype(BF16)
    nv = jnp.concatenate([nv_ref[0].astype(F32), nv_ref[1].astype(F32), fresh_pad], axis=0).astype(BF16)
    fresh = dot_nt(q_own, nk) * SCALING
    row, col = iota(fresh.shape, 0), iota(fresh.shape, 1)
    seen = (col // 2 == row // 16) & (col % 2 <= (row // 8) % 2)
    fresh = jnp.where(seen, fresh, NEG)
    own_peak = jnp.maximum(jnp.max(past, axis=1, keepdims=True), jnp.max(fresh, axis=1, keepdims=True))
    past_w = jnp.exp(past - own_peak).astype(BF16)
    fresh_w = jnp.exp(fresh - own_peak).astype(BF16)
    own_total = jnp.sum(past_w.astype(F32), axis=1, keepdims=True) + jnp.sum(
        fresh_w.astype(F32), axis=1, keepdims=True
    )
    own_part = jnp.where(first, dot(past_w, cv[0]), dot(past_w, cv[1])) + dot(fresh_w, nv)

    prompt = group_prompt_ref[chip // 2]
    length = prompt_len_ref[prompt]
    prompts = jnp.broadcast_to(cont_prompt_ref[...].astype(F32), (8, 128)).astype(BF16)
    for g in range(NX):
        lane = iota((128, 256), 1)
        cont = (g * NZ + lane // ROWS) * 4 + c * 2 + (lane % ROWS) // 16
        spread = jnp.where(iota((128, 256), 0) == cont, 1.0, 0.0).astype(BF16)
        prompt_of = dot(prompts, spread)
        member[g] = jnp.where(prompt_of == jnp.full((8, 256), prompt, jnp.int32).astype(F32), 1.0, 0.0)

    pl.semaphore_wait(barrier, CHIPS - 1 + 15)

    def q_copy(k):
        block = q_all.at[chip]
        return remote(block, block, q_ss.at[k], q_rs.at[k], lax.rem(chip + k, CHIPS), y, c)

    loop(1, CHIPS, lambda k: q_copy(k).start())
    swaps = [
        remote(src, dst, swap_ss.at[n], swap_rs.at[n], chip, y, other)
        for n, (src, dst) in enumerate(
            [
                (pk_in, pk.at[c]),
                (pv_in, pv.at[c]),
                (sk_in, sk.at[c]),
                (sv_in, sv.at[c]),
                (w_in, wt.at[c, pl.ds(0, 80)]),
            ]
        )
    ]
    for copy in swaps:
        copy.start()
    for copy in local[3:]:
        copy.wait()
    pvt[c] = with_ones(pv[c])
    svt[c] = with_ones(sv[c])
    for copy in swaps:
        copy.wait_recv()
    pvt[other] = with_ones(pv[other])
    svt[other] = with_ones(sv[other])

    def group_partial(g, put):
        rows = q_all[pl.ds(g * NZ, NZ)].reshape(NZ * ROWS, HD)
        mine = member[g][0:1] > 0.5
        peaks, parts = [], []
        for b in range(2):
            scores = dot_nt(pk[b], rows) * SCALING
            peak = jnp.max(scores, axis=0, keepdims=True)
            weights = jnp.exp(scores - peak).astype(BF16)
            peaks.append(peak)
            parts.append(dot(pvt[b], weights))
        for b in range(2):
            scores = dot_nt(sk[b], rows) * SCALING
            place = ((z % 2) * 2 + b) * 512 + iota((512, 1), 0)
            scores = jnp.where(place < length, scores, NEG)
            peak = jnp.max(scores, axis=0, keepdims=True)
            weights = jnp.exp(scores - peak).astype(BF16)
            peaks.append(jnp.where(mine, peak, NEG))
            parts.append(dot(svt[b], weights))
        put(*join(peaks, parts))

    def join(peaks, parts):
        top = functools.reduce(jnp.maximum, peaks)
        total = None
        for peak, part in zip(peaks, parts):
            term = jnp.exp(peak - top) * part[0:136]
            total = term if total is None else total + term
        stats = jnp.where(iota((8, 256), 0) == 1, top, total[128:136])
        return total[0:128], stats

    def x_copy(k):
        to = lax.rem(x + k, NX)
        return remote(x_send.at[to], x_recv.at[x], x_ss.at[k], x_rs.at[k], to * NZ + z, y, c)

    def q_wait(g):
        def one(n):
            k = lax.rem(chip - (g * NZ + n) + CHIPS, CHIPS)

            @pl.when(k > 0)
            def _():
                q_copy(k).wait_recv()

        loop(0, NZ, one)

    def group_step(k):
        g = lax.rem(x + k, NX)
        q_wait(g)

        def put_send(part, stats):
            x_send[g, 0:128] = part
            x_send[g, 128:136] = stats

        group_partial(g, put_send)
        x_copy(k).start()

    loop(1, NX, group_step)
    q_wait(x)

    def put_own(part, stats):
        x_recv[x, 0:128] = part
        x_recv[x, 128:136] = stats

    group_partial(x, put_own)
    loop(1, NX, lambda k: x_copy(k).wait_recv())

    part, stats = join([x_recv[s, 129:130] for s in range(NX)], [x_recv[s] for s in range(NX)])
    by_row = jnp.transpose(part)
    for t in range(NZ):
        half = stats[:, (t // 4) * 128 : (t // 4 + 1) * 128]
        turned = half if t % 4 == 0 else pltpu.roll(half, 128 - (t % 4) * ROWS, 1)
        z_send[t, 0:ROWS] = by_row[t * ROWS : (t + 1) * ROWS]
        z_send[t, ROWS : ROWS + 8] = turned
    z_recv[z] = z_send[z]

    def z_copy(k):
        to = lax.rem(z + k, NZ)
        return remote(z_send.at[to], z_recv.at[z], z_ss.at[k], z_rs.at[k], x * NZ + to, y, c)

    loop(1, NZ, lambda k: z_copy(k).start())
    loop(1, NZ, lambda k: z_copy(k).wait_recv())

    side = jnp.concatenate(
        [z_recv[s, ROWS + 1 : ROWS + 2] for s in range(NZ)]
        + [z_recv[s, ROWS : ROWS + 1] for s in range(NZ)]
        + [jnp.zeros((112, 128), F32)],
        axis=0,
    )
    side = jnp.transpose(side)[0:ROWS]
    top = jnp.maximum(jnp.max(side[:, 0:NZ], axis=1, keepdims=True), own_peak)
    own_factor = jnp.exp(own_peak - top)
    total, weighted = own_factor * own_total, own_factor * own_part
    for s in range(NZ):
        factor = jnp.exp(side[:, s : s + 1] - top)
        total = total + factor * side[:, NZ + s : NZ + s + 1]
        weighted = weighted + factor * z_recv[s, 0:ROWS]
    att[chip] = (weighted / total).astype(BF16)

    def a_copy(k):
        block = att.at[chip]
        return remote(block, block, a_ss.at[k], a_rs.at[k], lax.rem(chip + k, CHIPS), y, c)

    loop(1, CHIPS, lambda k: a_copy(k).start())
    loop(1, CHIPS, lambda k: a_copy(k).wait_recv())

    att_f32[...] = att[...].reshape(CHIPS * ROWS, HD).astype(F32)
    for h in range(GROUP):
        flat[:, h * HD : (h + 1) * HD] = att_f32[pl.ds(h, 128, stride=GROUP), :].astype(BF16)
    for b in range(2):
        y_send[b] = dot_nt(flat[...], wt[b]).reshape(NY, 16, 128)
    y_recv[yc] = y_send[c, y]

    def y_copy(k):
        to = lax.rem(yc + k, 16)
        return remote(
            y_send.at[to % 2, to // 2], y_recv.at[yc], y_ss.at[k], y_rs.at[k], chip, to // 2, to % 2
        )

    loop(1, 16, lambda k: y_copy(k).start())
    loop(1, 16, lambda k: y_copy(k).wait_recv())
    for b in range(2):
        summed = functools.reduce(jnp.add, [y_recv[n * 2 + b] for n in range(NY)])
        for n in range(4):
            for i in range(2):
                out_ref[n * 4 + b * 2 + i] = summed[n * 4 + i * 2 : n * 4 + i * 2 + 2, 0:80]

    for copy in swaps:
        copy.wait_send()
    loop(1, CHIPS, lambda k: q_copy(k).wait_send())
    loop(1, NX, lambda k: x_copy(k).wait_send())
    loop(1, NZ, lambda k: z_copy(k).wait_send())
    loop(1, CHIPS, lambda k: a_copy(k).wait_send())
    loop(1, 16, lambda k: y_copy(k).wait_send())


def body(
    queries,
    new_keys,
    new_values,
    prefix_keys,
    prefix_values,
    prompt_keys,
    prompt_values,
    cache_keys,
    cache_values,
    group_prompt,
    prompt_len,
    cont_prompt,
    cont_len,
    out_weight,
):
    anywhere = pl.BlockSpec(memory_space=pl.ANY)
    vmem = pl.BlockSpec(memory_space=pltpu.VMEM)
    smem = pl.BlockSpec(memory_space=pltpu.SMEM)
    dma = pltpu.SemaphoreType.DMA
    return pl.pallas_call(
        kernel,
        out_shape=jax.ShapeDtypeStruct((16, 2, 80), F32),
        in_specs=[anywhere] * 8 + [vmem] * 3 + [smem] * 3,
        out_specs=vmem,
        scratch_shapes=[
            pltpu.VMEM((CHIPS, ROWS, HD), BF16),
            pltpu.VMEM((2, 256, HD), BF16),
            pltpu.VMEM((2, 256, HD), BF16),
            pltpu.VMEM((2, 512, HD), BF16),
            pltpu.VMEM((2, 512, HD), BF16),
            pltpu.VMEM((2, 256, HD), BF16),
            pltpu.VMEM((2, 256, HD), BF16),
            pltpu.VMEM((2, 128, 1024), BF16),
            pltpu.VMEM((2, 144, 256), BF16),
            pltpu.VMEM((2, 144, 512), BF16),
            pltpu.VMEM((NX, 8, 256), F32),
            pltpu.VMEM((NX, 136, 256), F32),
            pltpu.VMEM((NX, 136, 256), F32),
            pltpu.VMEM((NZ, 40, 128), F32),
            pltpu.VMEM((NZ, 40, 128), F32),
            pltpu.VMEM((CHIPS, ROWS, HD), BF16),
            pltpu.VMEM((CHIPS * ROWS, HD), F32),
            pltpu.VMEM((128, 1024), BF16),
            pltpu.VMEM((2, NY, 16, 128), F32),
            pltpu.VMEM((16, 16, 128), F32),
            dma((8,)),
            dma((5,)),
            dma((5,)),
            dma((CHIPS,)),
            dma((CHIPS,)),
            dma((NX,)),
            dma((NX,)),
            dma((NZ,)),
            dma((NZ,)),
            dma((CHIPS,)),
            dma((CHIPS,)),
            dma((16,)),
            dma((16,)),
        ],
        compiler_params=pltpu.CompilerParams(
            collective_id=0, has_side_effects=True, vmem_limit_bytes=32 << 20
        ),
    )(
        queries.reshape(ROWS, HD),
        prefix_keys[:, 0, :],
        prefix_values[:, 0, :],
        prompt_keys[:, 0, :],
        prompt_values[:, 0, :],
        cache_keys[:, :, 0, :],
        cache_values[:, :, 0, :],
        out_weight.T,
        new_keys[:, :, 0, :],
        new_values[:, :, 0, :],
        cont_prompt.reshape(1, 128),
        group_prompt,
        prompt_len,
        cont_len,
    )


def solution(mesh):
    in_specs = (
        P("seq", None, "kvh", None),
        P("seq", None, "kvh", None),
        P("seq", None, "kvh", None),
        P("seq", "kvh", None),
        P("seq", "kvh", None),
        P("seq", "kvh", None),
        P("seq", "kvh", None),
        P("seq", None, "kvh", None),
        P("seq", None, "kvh", None),
        P(),
        P(),
        P(),
        P("seq"),
        P("kvh", "seq"),
    )
    out_specs = P("kvh", None, "seq")
    return jax.shard_map(body, mesh=mesh, in_specs=in_specs, out_specs=out_specs, check_vma=False)
```

```python
import functools
import math

import jax
import jax.numpy as jnp
from jax import lax
from jax.experimental import pallas as pl
from jax.experimental.pallas import tpu as pltpu
from jax.sharding import PartitionSpec as P

NEG = -1e30
MESH = pl.DeviceIdType.MESH
F32, BF16 = jnp.float32, jnp.bfloat16
NX, NZ, NC, NY = 4, 8, 2, 8
CHIPS = NX * NZ
ROWS = 32
HD = 128
GROUP = 8
SCALING = 1.0 / math.sqrt(HD)


def dot(a, b):
    return jnp.dot(a, b, preferred_element_type=F32)


def dot_nt(a, b):
    return lax.dot_general(a, b, (((1,), (1,)), ((), ())), preferred_element_type=F32)


def iota(shape, axis):
    return lax.broadcasted_iota(jnp.int32, shape, axis)


def loop(low, high, step):
    def run(k, carry):
        step(k)
        return carry

    lax.fori_loop(low, high, run, 0)


def remote(src, dst, send_sem, recv_sem, chip, y, core):
    return pltpu.make_async_remote_copy(
        src_ref=src,
        dst_ref=dst,
        send_sem=send_sem,
        recv_sem=recv_sem,
        device_id={"seq": chip * 2 + core, "kvh": y},
        device_id_type=MESH,
    )


def with_ones(values):
    flipped = jnp.transpose(values.astype(F32))
    return jnp.concatenate([flipped, jnp.ones((16, values.shape[0]), F32)], axis=0).astype(BF16)


def swing(i, middle):
    return middle + (i + 1) // 2 * (1 - 2 * (i % 2))


def attend(keys, flipped, rows, visible=None):
    scores = dot_nt(keys, rows) * SCALING
    if visible is not None:
        scores = jnp.where(visible, scores, NEG)
    peak = jnp.max(scores, axis=0, keepdims=True)
    weights = jnp.exp(scores - peak).astype(BF16)
    return peak, dot(flipped, weights)[0:136]


def join(peaks, parts):
    top = functools.reduce(jnp.maximum, peaks)
    total = None
    for peak, part in zip(peaks, parts):
        term = jnp.exp(peak - top) * part
        total = term if total is None else total + term
    width = top.shape[1]
    stats = jnp.where(iota((8, width), 0) == 1, top, total[128:136])
    return total[0:128], stats


def kernel(
    q_in,
    pk_in,
    pv_in,
    sk_in,
    sv_in,
    ck_in,
    cv_in,
    w_in,
    nk_ref,
    nv_ref,
    cont_prompt_ref,
    group_prompt_ref,
    prompt_len_ref,
    cont_len_ref,
    out_ref,
    q_all,
    kv,
    sk,
    sv,
    ck,
    cv,
    wt,
    places,
    pick,
    spread,
    parts,
    x_recv,
    z_send,
    z_recv,
    att,
    att_f32,
    flat,
    y_send,
    y_recv,
    own_sem,
    swap_ss,
    swap_rs,
    kv_ss,
    kv_rs,
    fw_ss,
    fw_rs,
    q_ss,
    q_rs,
    x_ss,
    x_rs,
    z_ss,
    z_rs,
    a_ss,
    a_rs,
    y_ss,
    y_rs,
):
    seq = lax.axis_index("seq")
    y = lax.axis_index("kvh")
    chip, c = seq // 2, seq % 2
    x, z = chip // NZ, chip % NZ
    other = 1 - c
    yc = y * 2 + c

    barrier = pltpu.get_barrier_semaphore()

    def greet_plane(k):
        pl.semaphore_signal(
            barrier,
            inc=1,
            device_id={"seq": lax.rem(chip + k, CHIPS) * 2 + c, "kvh": y},
            device_id_type=MESH,
        )

    def greet_column(k):
        to = lax.rem(yc + k, 16)
        pl.semaphore_signal(
            barrier, inc=1, device_id={"seq": chip * 2 + to % 2, "kvh": to // 2}, device_id_type=MESH
        )

    loop(1, CHIPS, greet_plane)
    loop(1, 16, greet_column)

    local = [
        pltpu.make_async_copy(src, dst, own_sem.at[n])
        for n, (src, dst) in enumerate(
            [
                (q_in, q_all.at[chip]),
                (ck_in, ck),
                (cv_in, cv),
                (pk_in, kv.at[x, c, 0]),
                (pv_in, kv.at[x, c, 1]),
                (sk_in, sk.at[c]),
                (sv_in, sv.at[c]),
                (w_in, wt.at[c, pl.ds(0, 80)]),
            ]
        )
    ]
    for copy in local:
        copy.start()
    wt[:, 80:, :] = jnp.zeros((2, 48, wt.shape[2]), BF16)

    cont_prompt = cont_prompt_ref[...]
    conts = iota((1, 128), 1)
    on_core = (conts // 2) % 2 == c
    members = [
        jnp.where((cont_prompt == group_prompt_ref[(g * NZ + z) // 2]) & on_core, 1.0, 0.0)
        for g in range(NX)
    ]
    members = jnp.concatenate(members + [jnp.zeros((4, 128), F32)], axis=0)
    before = jnp.where(iota((128, 128), 0) < iota((128, 128), 1), 1.0, 0.0).astype(BF16)
    ranks = ((dot(members.astype(BF16), before) + 1.0) * members).astype(BF16)
    lane = iota((128, 256), 1)
    inside = (lane % 16).astype(F32)[0:8]
    for g in range(NX):
        cont = (g * NZ + lane // ROWS) * 4 + c * 2 + (lane % ROWS) // 16
        widen = jnp.where(iota((128, 256), 0) == cont, 1.0, 0.0).astype(BF16)
        ranked = dot(ranks, widen)
        places[g] = jnp.where(ranked > 0.5, ranked * 16.0 - 16.0 + inside, -1.0)
    place_row = iota((128, 256), 0).astype(F32)
    for g in range(NX):
        pick[g] = jnp.where(place_row == places[g, pl.ds(x, 1)], 1.0, 0.0).astype(BF16)
        spread[g] = jnp.where(place_row == places[x, pl.ds(g, 1)], 1.0, 0.0).astype(BF16)

    for copy in local[:3]:
        copy.wait()
    q_own = q_all[chip]
    first = iota((ROWS, 1), 0) < 16
    past0 = dot_nt(q_own, ck[0]) * SCALING
    past1 = dot_nt(q_own, ck[1]) * SCALING
    lengths = jnp.where(first, cont_len_ref[0], cont_len_ref[1])
    past = jnp.where(iota(past0.shape, 1) < lengths, jnp.where(first, past0, past1), NEG)
    fresh_pad = jnp.zeros((12, HD), F32)
    nk = jnp.concatenate([nk_ref[0].astype(F32), nk_ref[1].astype(F32), fresh_pad], axis=0).astype(BF16)
    nv = jnp.concatenate([nv_ref[0].astype(F32), nv_ref[1].astype(F32), fresh_pad], axis=0).astype(BF16)
    fresh = dot_nt(q_own, nk) * SCALING
    row, col = iota(fresh.shape, 0), iota(fresh.shape, 1)
    seen = (col // 2 == row // 16) & (col % 2 <= (row // 8) % 2)
    fresh = jnp.where(seen, fresh, NEG)
    own_peak = jnp.maximum(jnp.max(past, axis=1, keepdims=True), jnp.max(fresh, axis=1, keepdims=True))
    past_w = jnp.exp(past - own_peak).astype(BF16)
    fresh_w = jnp.exp(fresh - own_peak).astype(BF16)
    own_total = jnp.sum(past_w.astype(F32), axis=1, keepdims=True) + jnp.sum(
        fresh_w.astype(F32), axis=1, keepdims=True
    )
    own_part = jnp.where(first, dot(past_w, cv[0]), dot(past_w, cv[1])) + dot(fresh_w, nv)
    for copy in local[3:]:
        copy.wait()

    pl.semaphore_wait(barrier, CHIPS - 1 + 15)

    def chip_at(n):
        return lax.rem(x + n // NZ, NX) * NZ + lax.rem(z + n % NZ, NZ)

    def far_first(n):
        return swing(n // NZ, 2) * NZ + swing(n % NZ, 4)

    def q_copy(n):
        block = q_all.at[chip]
        return remote(block, block, q_ss.at[n], q_rs.at[n], chip_at(n), y, c)

    loop(0, CHIPS - 1, lambda n: q_copy(far_first(n)).start())

    def kv_copy(k):
        block = kv.at[x, c]
        return remote(block, block, kv_ss.at[k], kv_rs.at[k], lax.rem(x + k, NX) * NZ + z, y, c)

    def fw_copy(k):
        block = kv.at[lax.rem(x + NX - k, NX), c]
        return remote(block, block, fw_ss.at[k], fw_rs.at[k], chip, y, other)

    swaps = [
        remote(src, src, swap_ss.at[n], swap_rs.at[n], chip, y, other)
        for n, src in enumerate([sk.at[c], sv.at[c], wt.at[c, pl.ds(0, 80)]])
    ]
    for k in (2, 1, 3):
        kv_copy(k).start()
    fw_copy(0).start()
    for copy in swaps:
        copy.start()
    for k in (1, 3, 2):
        kv_copy(k).wait_recv()
        fw_copy(k).start()

    def rows_of(g):
        return q_all[pl.ds(g * NZ, NZ)].reshape(NZ * ROWS, HD)

    def prefix_block(n):
        block = kv.at[lax.rem(x + NX - n // 2, NX), lax.rem(c + n, 2)]
        peak, part = attend(block[0], with_ones(block[1]), rows_of(x))
        parts[n, 0:128] = part[0:128]
        parts[n, 128:136] = jnp.where(iota((8, 256), 0) == 1, peak, part[128:136])

    loop(1, NZ, lambda n: q_copy(n).wait_recv())
    fw_copy(0).wait_recv()
    loop(0, 2, prefix_block)

    for copy in swaps:
        copy.wait_recv()
    length = prompt_len_ref[group_prompt_ref[chip // 2]]
    flipped = [with_ones(sv[b]) for b in range(2)]
    loop(NZ, CHIPS, lambda n: q_copy(n).wait_recv())
    picked = functools.reduce(jnp.add, [dot(pick[g], rows_of(g)) for g in range(NX)]).astype(BF16)
    pairs = [
        attend(
            sk[b],
            flipped[b],
            picked,
            ((z % 2) * 2 + b) * 512 + iota((512, 1), 0) < length,
        )
        for b in range(2)
    ]
    part, stats = join([p[0] for p in pairs], [p[1] for p in pairs])
    x_recv[x, 0:128] = part
    x_recv[x, 128:136] = stats

    def x_copy(k):
        block = x_recv.at[x]
        return remote(block, block, x_ss.at[k], x_rs.at[k], lax.rem(x + k, NX) * NZ + z, y, c)

    for k in (2, 1, 3):
        x_copy(k).start()

    for k in range(1, NX):
        fw_copy(k).wait_recv()
    loop(2, 8, prefix_block)
    part, stats = join([parts[n, 129:130] for n in range(8)], [parts[n] for n in range(8)])
    for k in range(1, NX):
        x_copy(k).wait_recv()
    peaks, sums = [stats[1:2]], [jnp.concatenate([part, stats], axis=0)]
    for g in range(NX):
        compact = x_recv[g]
        high = compact.astype(BF16)
        rest = compact - high.astype(F32)
        middle = rest.astype(BF16)
        low = (rest - middle.astype(F32)).astype(BF16)
        wide = dot(high, spread[g]) + dot(middle, spread[g]) + dot(low, spread[g])
        peaks.append(jnp.where(places[x, pl.ds(g, 1)] >= 0.0, wide[129:130], NEG))
        sums.append(wide)
    part, stats = join(peaks, sums)

    by_row = jnp.transpose(part)
    for t in range(NZ):
        half = stats[:, (t // 4) * 128 : (t // 4 + 1) * 128]
        turned = half if t % 4 == 0 else pltpu.roll(half, 128 - (t % 4) * ROWS, 1)
        z_send[t, 0:ROWS] = by_row[t * ROWS : (t + 1) * ROWS]
        z_send[t, ROWS : ROWS + 8] = turned

    def z_copy(k):
        to = lax.rem(z + k, NZ)
        return remote(z_send.at[to], z_recv.at[z], z_ss.at[k], z_rs.at[k], x * NZ + to, y, c)

    loop(0, NZ - 1, lambda n: z_copy(swing(n, 4)).start())
    z_recv[z] = z_send[z]
    loop(1, NZ, lambda k: z_copy(k).wait_recv())

    side = jnp.concatenate(
        [z_recv[s, ROWS + 1 : ROWS + 2] for s in range(NZ)]
        + [z_recv[s, ROWS : ROWS + 1] for s in range(NZ)]
        + [jnp.zeros((112, 128), F32)],
        axis=0,
    )
    side = jnp.transpose(side)[0:ROWS]
    top = jnp.maximum(jnp.max(side[:, 0:NZ], axis=1, keepdims=True), own_peak)
    own_factor = jnp.exp(own_peak - top)
    total, weighted = own_factor * own_total, own_factor * own_part
    for s in range(NZ):
        factor = jnp.exp(side[:, s : s + 1] - top)
        total = total + factor * side[:, NZ + s : NZ + s + 1]
        weighted = weighted + factor * z_recv[s, 0:ROWS]
    att[chip] = (weighted / total).astype(BF16)

    def a_copy(n):
        block = att.at[chip]
        return remote(block, block, a_ss.at[n], a_rs.at[n], chip_at(n), y, c)

    loop(0, CHIPS - 1, lambda n: a_copy(far_first(n)).start())
    loop(1, CHIPS, lambda n: a_copy(n).wait_recv())

    att_f32[...] = att[...].reshape(CHIPS * ROWS, HD).astype(F32)
    for h in range(GROUP):
        flat[:, h * HD : (h + 1) * HD] = att_f32[pl.ds(h, 128, stride=GROUP), :].astype(BF16)
    for b in range(2):
        y_send[b] = dot_nt(flat[...], wt[b]).reshape(NY, 16, 128)
    y_recv[yc] = y_send[c, y]

    def y_copy(n):
        to_y, to_c = lax.rem(y + n // 2, NY), lax.rem(c + n, 2)
        return remote(
            y_send.at[to_c, to_y], y_recv.at[yc], y_ss.at[n], y_rs.at[n], chip, to_y, to_c
        )

    loop(0, 15, lambda n: y_copy(swing(n // 2, 4) * 2 + 1 - n % 2).start())
    loop(1, 16, lambda n: y_copy(n).wait_recv())
    for b in range(2):
        summed = functools.reduce(jnp.add, [y_recv[n * 2 + b] for n in range(NY)])
        for n in range(4):
            for i in range(2):
                out_ref[n * 4 + b * 2 + i] = summed[n * 4 + i * 2 : n * 4 + i * 2 + 2, 0:80]

    for copy in swaps:
        copy.wait_send()
    for k in range(NX):
        fw_copy(k).wait_send()
    for k in range(1, NX):
        kv_copy(k).wait_send()
        x_copy(k).wait_send()
    loop(1, CHIPS, lambda n: q_copy(n).wait_send())
    loop(1, NZ, lambda k: z_copy(k).wait_send())
    loop(1, CHIPS, lambda n: a_copy(n).wait_send())
    loop(1, 16, lambda n: y_copy(n).wait_send())


def body(
    queries,
    new_keys,
    new_values,
    prefix_keys,
    prefix_values,
    prompt_keys,
    prompt_values,
    cache_keys,
    cache_values,
    group_prompt,
    prompt_len,
    cont_prompt,
    cont_len,
    out_weight,
):
    anywhere = pl.BlockSpec(memory_space=pl.ANY)
    vmem = pl.BlockSpec(memory_space=pltpu.VMEM)
    smem = pl.BlockSpec(memory_space=pltpu.SMEM)
    dma = pltpu.SemaphoreType.DMA
    return pl.pallas_call(
        kernel,
        out_shape=jax.ShapeDtypeStruct((16, 2, 80), F32),
        in_specs=[anywhere] * 8 + [vmem] * 3 + [smem] * 3,
        out_specs=vmem,
        scratch_shapes=[
            pltpu.VMEM((CHIPS, ROWS, HD), BF16),
            pltpu.VMEM((NX, 2, 2, 256, HD), BF16),
            pltpu.VMEM((2, 512, HD), BF16),
            pltpu.VMEM((2, 512, HD), BF16),
            pltpu.VMEM((2, 256, HD), BF16),
            pltpu.VMEM((2, 256, HD), BF16),
            pltpu.VMEM((2, 128, 1024), BF16),
            pltpu.VMEM((NX, 8, 256), F32),
            pltpu.VMEM((NX, 128, 256), BF16),
            pltpu.VMEM((NX, 128, 256), BF16),
            pltpu.VMEM((8, 136, 256), F32),
            pltpu.VMEM((NX, 136, 128), F32),
            pltpu.VMEM((NZ, 40, 128), F32),
            pltpu.VMEM((NZ, 40, 128), F32),
            pltpu.VMEM((CHIPS, ROWS, HD), BF16),
            pltpu.VMEM((CHIPS * ROWS, HD), F32),
            pltpu.VMEM((128, 1024), BF16),
            pltpu.VMEM((2, NY, 16, 128), F32),
            pltpu.VMEM((16, 16, 128), F32),
            dma((8,)),
            dma((3,)),
            dma((3,)),
            dma((NX,)),
            dma((NX,)),
            dma((NX,)),
            dma((NX,)),
            dma((CHIPS,)),
            dma((CHIPS,)),
            dma((NX,)),
            dma((NX,)),
            dma((NZ,)),
            dma((NZ,)),
            dma((CHIPS,)),
            dma((CHIPS,)),
            dma((16,)),
            dma((16,)),
        ],
        compiler_params=pltpu.CompilerParams(
            collective_id=0, has_side_effects=True, vmem_limit_bytes=60 << 20
        ),
    )(
        queries.reshape(ROWS, HD),
        prefix_keys[:, 0, :],
        prefix_values[:, 0, :],
        prompt_keys[:, 0, :],
        prompt_values[:, 0, :],
        cache_keys[:, :, 0, :],
        cache_values[:, :, 0, :],
        out_weight.T,
        new_keys[:, :, 0, :],
        new_values[:, :, 0, :],
        cont_prompt.reshape(1, 128),
        group_prompt,
        prompt_len,
        cont_len,
    )


def solution(mesh):
    in_specs = (
        P("seq", None, "kvh", None),
        P("seq", None, "kvh", None),
        P("seq", None, "kvh", None),
        P("seq", "kvh", None),
        P("seq", "kvh", None),
        P("seq", "kvh", None),
        P("seq", "kvh", None),
        P("seq", None, "kvh", None),
        P("seq", None, "kvh", None),
        P(),
        P(),
        P(),
        P("seq"),
        P("kvh", "seq"),
    )
    out_specs = P("kvh", None, "seq")
    return jax.shard_map(body, mesh=mesh, in_specs=in_specs, out_specs=out_specs, check_vma=False)
```

```python
import functools
import math

import jax
import jax.numpy as jnp
from jax import lax
from jax.experimental import pallas as pl
from jax.experimental.pallas import tpu as pltpu
from jax.sharding import PartitionSpec as P

NEG = -1e30
MESH = pl.DeviceIdType.MESH
F32, BF16 = jnp.float32, jnp.bfloat16
NX, NZ, NC, NY = 4, 8, 2, 8
CHIPS = NX * NZ
ROWS = 32
HD = 128
GROUP = 8
SCALING = 1.0 / math.sqrt(HD)


def dot(a, b):
    return jnp.dot(a, b, preferred_element_type=F32)


def dot_nt(a, b):
    return lax.dot_general(a, b, (((1,), (1,)), ((), ())), preferred_element_type=F32)


def iota(shape, axis):
    return lax.broadcasted_iota(jnp.int32, shape, axis)


def loop(low, high, step):
    def run(k, carry):
        step(k)
        return carry

    lax.fori_loop(low, high, run, 0)


def remote(src, dst, send_sem, recv_sem, chip, y, core):
    return pltpu.make_async_remote_copy(
        src_ref=src,
        dst_ref=dst,
        send_sem=send_sem,
        recv_sem=recv_sem,
        device_id={"seq": chip * 2 + core, "kvh": y},
        device_id_type=MESH,
    )


def with_ones(values):
    flipped = jnp.transpose(values.astype(F32))
    return jnp.concatenate([flipped, jnp.ones((16, values.shape[0]), F32)], axis=0).astype(BF16)


X_STEPS, Z_STEPS, Y_STEPS = (2, 1, 3, 0), (4, 3, 5, 2, 6, 1, 7, 0), (4, 3, 5, 2, 6, 1, 7, 0)
FAR_FIRST = [(dx, dz) for dx in X_STEPS for dz in Z_STEPS if dx or dz]


def attend(keys, flipped, rows, visible=None):
    scores = dot_nt(keys, rows) * SCALING
    if visible is not None:
        scores = jnp.where(visible, scores, NEG)
    peak = jnp.max(scores, axis=0, keepdims=True)
    weights = jnp.exp(scores - peak).astype(BF16)
    return peak, dot(flipped, weights)[0:136]


def join(peaks, parts):
    top = functools.reduce(jnp.maximum, peaks)
    total = None
    for peak, part in zip(peaks, parts):
        term = jnp.exp(peak - top) * part
        total = term if total is None else total + term
    width = top.shape[1]
    stats = jnp.where(iota((8, width), 0) == 1, top, total[128:136])
    return total[0:128], stats


def kernel(
    q_in,
    pk_in,
    pv_in,
    sk_in,
    sv_in,
    ck_in,
    cv_in,
    w_in,
    nk_ref,
    nv_ref,
    cont_prompt_ref,
    group_prompt_ref,
    prompt_len_ref,
    cont_len_ref,
    out_ref,
    q_all,
    kv,
    sk,
    sv,
    ck,
    cv,
    wt,
    places,
    pick,
    spread,
    parts,
    x_recv,
    z_send,
    z_recv,
    att,
    att_f32,
    flat,
    y_send,
    y_recv,
    own_sem,
    swap_ss,
    swap_rs,
    kv_ss,
    kv_rs,
    fw_ss,
    fw_rs,
    q_ss,
    q_rs,
    x_ss,
    x_rs,
    z_ss,
    z_rs,
    a_ss,
    a_rs,
    y_ss,
    y_rs,
):
    seq = lax.axis_index("seq")
    y = lax.axis_index("kvh")
    chip, c = seq // 2, seq % 2
    x, z = chip // NZ, chip % NZ
    other = 1 - c
    yc = y * 2 + c

    barrier = pltpu.get_barrier_semaphore()

    x_to = [lax.rem(x + d, NX) * NZ for d in range(NX)]
    z_to = [lax.rem(z + d, NZ) for d in range(NZ)]
    y_to = [lax.rem(y + d, NY) for d in range(NY)]

    def greet(to_chip, to_y, to_c):
        pl.semaphore_signal(
            barrier, inc=1, device_id={"seq": to_chip * 2 + to_c, "kvh": to_y}, device_id_type=MESH
        )

    for dx, dz in FAR_FIRST:
        greet(x_to[dx] + z_to[dz], y, c)
    for dy in Y_STEPS:
        greet(chip, y_to[dy], other)
        if dy:
            greet(chip, y_to[dy], c)

    local = [
        pltpu.make_async_copy(src, dst, own_sem.at[n])
        for n, (src, dst) in enumerate(
            [
                (q_in, q_all.at[chip]),
                (ck_in, ck),
                (cv_in, cv),
                (pk_in, kv.at[x, c, 0]),
                (pv_in, kv.at[x, c, 1]),
                (sk_in, sk.at[c]),
                (sv_in, sv.at[c]),
                (w_in, wt.at[c, pl.ds(0, 80)]),
            ]
        )
    ]
    for copy in local:
        copy.start()
    wt[:, 80:, :] = jnp.zeros((2, 48, wt.shape[2]), BF16)

    for copy in local:
        copy.wait()

    pl.semaphore_wait(barrier, CHIPS - 1 + 15)

    def q_copy(dx, dz):
        block = q_all.at[chip]
        return remote(block, block, q_ss, q_rs.at[1 if dx else 0], x_to[dx] + z_to[dz], y, c)

    for dx, dz in FAR_FIRST:
        q_copy(dx, dz).start()

    def kv_copy(k):
        block = kv.at[x, c]
        return remote(block, block, kv_ss.at[k], kv_rs.at[k], x_to[k] + z, y, c)

    def fw_copy(k):
        block = kv.at[lax.rem(x + NX - k, NX), c]
        return remote(block, block, fw_ss.at[k], fw_rs.at[k], chip, y, other)

    swaps = [
        remote(src, src, swap_ss.at[n], swap_rs.at[n], chip, y, other)
        for n, src in enumerate([sk.at[c], sv.at[c], wt.at[c, pl.ds(0, 80)]])
    ]
    for k in (2, 1, 3):
        kv_copy(k).start()
    fw_copy(0).start()
    for copy in swaps:
        copy.start()

    cont_prompt = cont_prompt_ref[...]
    conts = iota((1, 128), 1)
    on_core = (conts // 2) % 2 == c
    members = [
        jnp.where((cont_prompt == group_prompt_ref[(g * NZ + z) // 2]) & on_core, 1.0, 0.0)
        for g in range(NX)
    ]
    members = jnp.concatenate(members + [jnp.zeros((4, 128), F32)], axis=0)
    before = jnp.where(iota((128, 128), 0) < iota((128, 128), 1), 1.0, 0.0).astype(BF16)
    ranks = ((dot(members.astype(BF16), before) + 1.0) * members).astype(BF16)
    lane = iota((128, 256), 1)
    inside = (lane % 16).astype(F32)[0:8]
    for g in range(NX):
        cont = (g * NZ + lane // ROWS) * 4 + c * 2 + (lane % ROWS) // 16
        widen = jnp.where(iota((128, 256), 0) == cont, 1.0, 0.0).astype(BF16)
        ranked = dot(ranks, widen)
        places[g] = jnp.where(ranked > 0.5, ranked * 16.0 - 16.0 + inside, -1.0)
    place_row = iota((128, 256), 0).astype(F32)
    for g in range(NX):
        pick[g] = jnp.where(place_row == places[g, pl.ds(x, 1)], 1.0, 0.0).astype(BF16)
        spread[g] = jnp.where(place_row == places[x, pl.ds(g, 1)], 1.0, 0.0).astype(BF16)

    q_own = q_all[chip]
    first = iota((ROWS, 1), 0) < 16
    past0 = dot_nt(q_own, ck[0]) * SCALING
    past1 = dot_nt(q_own, ck[1]) * SCALING
    lengths = jnp.where(first, cont_len_ref[0], cont_len_ref[1])
    past = jnp.where(iota(past0.shape, 1) < lengths, jnp.where(first, past0, past1), NEG)
    fresh_pad = jnp.zeros((12, HD), F32)
    nk = jnp.concatenate([nk_ref[0].astype(F32), nk_ref[1].astype(F32), fresh_pad], axis=0).astype(BF16)
    nv = jnp.concatenate([nv_ref[0].astype(F32), nv_ref[1].astype(F32), fresh_pad], axis=0).astype(BF16)
    fresh = dot_nt(q_own, nk) * SCALING
    row, col = iota(fresh.shape, 0), iota(fresh.shape, 1)
    seen = (col // 2 == row // 16) & (col % 2 <= (row // 8) % 2)
    fresh = jnp.where(seen, fresh, NEG)
    own_peak = jnp.maximum(jnp.max(past, axis=1, keepdims=True), jnp.max(fresh, axis=1, keepdims=True))
    past_w = jnp.exp(past - own_peak).astype(BF16)
    fresh_w = jnp.exp(fresh - own_peak).astype(BF16)
    own_total = jnp.sum(past_w.astype(F32), axis=1, keepdims=True) + jnp.sum(
        fresh_w.astype(F32), axis=1, keepdims=True
    )
    own_part = jnp.where(first, dot(past_w, cv[0]), dot(past_w, cv[1])) + dot(fresh_w, nv)
    def arrived(ref, sem):
        remote(ref, ref, q_ss, sem, chip, y, other).wait_recv()

    def left(ref, sem):
        remote(ref, ref, sem, q_rs.at[0], chip, y, other).wait_send()

    for k in (1, 3, 2):
        kv_copy(k).wait_recv()
        fw_copy(k).start()

    def rows_of(g):
        return q_all[pl.ds(g * NZ, NZ)].reshape(NZ * ROWS, HD)

    def prefix_block(n):
        block = kv.at[lax.rem(x + NX - n // 2, NX), lax.rem(c + n, 2)]
        peak, part = attend(block[0], with_ones(block[1]), rows_of(x))
        parts[n, 0:128] = part[0:128]
        parts[n, 128:136] = jnp.where(iota((8, 256), 0) == 1, peak, part[128:136])

    arrived(q_all.at[pl.ds(0, NZ - 1)], q_rs.at[0])
    fw_copy(0).wait_recv()
    loop(0, 2, prefix_block)

    for copy in swaps:
        copy.wait_recv()
    length = prompt_len_ref[group_prompt_ref[chip // 2]]
    flipped = [with_ones(sv[b]) for b in range(2)]
    arrived(q_all.at[pl.ds(0, CHIPS - NZ)], q_rs.at[1])
    picked = functools.reduce(jnp.add, [dot(pick[g], rows_of(g)) for g in range(NX)]).astype(BF16)
    pairs = [
        attend(
            sk[b],
            flipped[b],
            picked,
            ((z % 2) * 2 + b) * 512 + iota((512, 1), 0) < length,
        )
        for b in range(2)
    ]
    part, stats = join([p[0] for p in pairs], [p[1] for p in pairs])
    x_recv[x, 0:128] = part
    x_recv[x, 128:136] = stats

    def x_copy(k):
        block = x_recv.at[x]
        return remote(block, block, x_ss.at[k], x_rs.at[k], x_to[k] + z, y, c)

    for k in (2, 1, 3):
        x_copy(k).start()

    for k in range(1, NX):
        fw_copy(k).wait_recv()
    loop(2, 8, prefix_block)
    part, stats = join([parts[n, 129:130] for n in range(8)], [parts[n] for n in range(8)])
    left(q_all.at[pl.ds(0, CHIPS - 1)], q_ss)
    for copy in swaps:
        copy.wait_send()
    for k in range(NX):
        fw_copy(k).wait_send()
    for k in range(1, NX):
        kv_copy(k).wait_send()
    for k in range(1, NX):
        x_copy(k).wait_recv()
    peaks, sums = [stats[1:2]], [jnp.concatenate([part, stats], axis=0)]
    for g in range(NX):
        compact = x_recv[g]
        high = compact.astype(BF16)
        rest = compact - high.astype(F32)
        middle = rest.astype(BF16)
        low = (rest - middle.astype(F32)).astype(BF16)
        wide = dot(high, spread[g]) + dot(middle, spread[g]) + dot(low, spread[g])
        peaks.append(jnp.where(places[x, pl.ds(g, 1)] >= 0.0, wide[129:130], NEG))
        sums.append(wide)
    part, stats = join(peaks, sums)

    by_row = jnp.transpose(part)
    for t in range(NZ):
        half = stats[:, (t // 4) * 128 : (t // 4 + 1) * 128]
        turned = half if t % 4 == 0 else pltpu.roll(half, 128 - (t % 4) * ROWS, 1)
        z_send[t, 0:ROWS] = by_row[t * ROWS : (t + 1) * ROWS]
        z_send[t, ROWS : ROWS + 8] = turned

    for dz in Z_STEPS[:-1]:
        to = z_to[dz]
        remote(z_send.at[to], z_recv.at[z], z_ss, z_rs, x_to[0] + to, y, c).start()
    z_recv[z] = z_send[z]
    for k in range(1, NX):
        x_copy(k).wait_send()
    arrived(z_recv.at[pl.ds(0, NZ - 1)], z_rs)

    side = jnp.concatenate(
        [z_recv[s, ROWS + 1 : ROWS + 2] for s in range(NZ)]
        + [z_recv[s, ROWS : ROWS + 1] for s in range(NZ)]
        + [jnp.zeros((112, 128), F32)],
        axis=0,
    )
    side = jnp.transpose(side)[0:ROWS]
    top = jnp.maximum(jnp.max(side[:, 0:NZ], axis=1, keepdims=True), own_peak)
    own_factor = jnp.exp(own_peak - top)
    total, weighted = own_factor * own_total, own_factor * own_part
    for s in range(NZ):
        factor = jnp.exp(side[:, s : s + 1] - top)
        total = total + factor * side[:, NZ + s : NZ + s + 1]
        weighted = weighted + factor * z_recv[s, 0:ROWS]
    att[chip] = (weighted / total).astype(BF16)

    for dx, dz in FAR_FIRST:
        block = att.at[chip]
        remote(block, block, a_ss, a_rs, x_to[dx] + z_to[dz], y, c).start()
    left(z_send.at[pl.ds(0, NZ - 1)], z_ss)
    arrived(att.at[pl.ds(0, CHIPS - 1)], a_rs)

    att_f32[...] = att[...].reshape(CHIPS * ROWS, HD).astype(F32)
    for h in range(GROUP):
        flat[:, h * HD : (h + 1) * HD] = att_f32[pl.ds(h, 128, stride=GROUP), :].astype(BF16)
    for b in range(2):
        y_send[b] = dot_nt(flat[...], wt[b]).reshape(NY, 16, 128)
    for dy in Y_STEPS:
        for dc in (1, 0):
            if dy or dc:
                to_y, to_c = y_to[dy], other if dc else c
                remote(y_send.at[to_c, to_y], y_recv.at[yc], y_ss, y_rs, chip, to_y, to_c).start()
    y_recv[yc] = y_send[c, y]
    left(att.at[pl.ds(0, CHIPS - 1)], a_ss)
    arrived(y_recv.at[pl.ds(0, 15)], y_rs)
    for b in range(2):
        summed = functools.reduce(jnp.add, [y_recv[n * 2 + b] for n in range(NY)])
        for n in range(4):
            for i in range(2):
                out_ref[n * 4 + b * 2 + i] = summed[n * 4 + i * 2 : n * 4 + i * 2 + 2, 0:80]

    left(y_recv.at[pl.ds(0, 15)], y_ss)


def body(
    queries,
    new_keys,
    new_values,
    prefix_keys,
    prefix_values,
    prompt_keys,
    prompt_values,
    cache_keys,
    cache_values,
    group_prompt,
    prompt_len,
    cont_prompt,
    cont_len,
    out_weight,
):
    anywhere = pl.BlockSpec(memory_space=pl.ANY)
    vmem = pl.BlockSpec(memory_space=pltpu.VMEM)
    smem = pl.BlockSpec(memory_space=pltpu.SMEM)
    dma = pltpu.SemaphoreType.DMA
    return pl.pallas_call(
        kernel,
        out_shape=jax.ShapeDtypeStruct((16, 2, 80), F32),
        in_specs=[anywhere] * 8 + [vmem] * 3 + [smem] * 3,
        out_specs=vmem,
        scratch_shapes=[
            pltpu.VMEM((CHIPS, ROWS, HD), BF16),
            pltpu.VMEM((NX, 2, 2, 256, HD), BF16),
            pltpu.VMEM((2, 512, HD), BF16),
            pltpu.VMEM((2, 512, HD), BF16),
            pltpu.VMEM((2, 256, HD), BF16),
            pltpu.VMEM((2, 256, HD), BF16),
            pltpu.VMEM((2, 128, 1024), BF16),
            pltpu.VMEM((NX, 8, 256), F32),
            pltpu.VMEM((NX, 128, 256), BF16),
            pltpu.VMEM((NX, 128, 256), BF16),
            pltpu.VMEM((8, 136, 256), F32),
            pltpu.VMEM((NX, 136, 128), F32),
            pltpu.VMEM((NZ, 40, 128), F32),
            pltpu.VMEM((NZ, 40, 128), F32),
            pltpu.VMEM((CHIPS, ROWS, HD), BF16),
            pltpu.VMEM((CHIPS * ROWS, HD), F32),
            pltpu.VMEM((128, 1024), BF16),
            pltpu.VMEM((2, NY, 16, 128), F32),
            pltpu.VMEM((16, 16, 128), F32),
            dma((8,)),
            dma((3,)),
            dma((3,)),
            dma((NX,)),
            dma((NX,)),
            dma((NX,)),
            dma((NX,)),
            dma,
            dma((2,)),
            dma((NX,)),
            dma((NX,)),
            dma,
            dma,
            dma,
            dma,
            dma,
            dma,
        ],
        compiler_params=pltpu.CompilerParams(
            collective_id=0, has_side_effects=True, vmem_limit_bytes=55168 << 10
        ),
    )(
        queries.reshape(ROWS, HD),
        prefix_keys[:, 0, :],
        prefix_values[:, 0, :],
        prompt_keys[:, 0, :],
        prompt_values[:, 0, :],
        cache_keys[:, :, 0, :],
        cache_values[:, :, 0, :],
        out_weight.T,
        new_keys[:, :, 0, :],
        new_values[:, :, 0, :],
        cont_prompt.reshape(1, 128),
        group_prompt,
        prompt_len,
        cont_len,
    )


def solution(mesh):
    in_specs = (
        P("seq", None, "kvh", None),
        P("seq", None, "kvh", None),
        P("seq", None, "kvh", None),
        P("seq", "kvh", None),
        P("seq", "kvh", None),
        P("seq", "kvh", None),
        P("seq", "kvh", None),
        P("seq", None, "kvh", None),
        P("seq", None, "kvh", None),
        P(),
        P(),
        P(),
        P("seq"),
        P("kvh", "seq"),
    )
    out_specs = P("kvh", None, "seq")
    return jax.shard_map(body, mesh=mesh, in_specs=in_specs, out_specs=out_specs, check_vma=False)
```

```python
import functools
import math

import jax
import jax.numpy as jnp
from jax import lax
from jax.experimental import pallas as pl
from jax.experimental.pallas import tpu as pltpu
from jax.sharding import PartitionSpec as P

NEG = -1e30
MESH = pl.DeviceIdType.MESH
F32, BF16 = jnp.float32, jnp.bfloat16
NX, NZ, NC, NY = 4, 8, 2, 8
CHIPS = NX * NZ
ROWS = 32
HD = 128
GROUP = 8
SCALING = 1.0 / math.sqrt(HD)


def dot(a, b):
    return jnp.dot(a, b, preferred_element_type=F32)


def dot_nt(a, b):
    return lax.dot_general(a, b, (((1,), (1,)), ((), ())), preferred_element_type=F32)


def iota(shape, axis):
    return lax.broadcasted_iota(jnp.int32, shape, axis)


def loop(low, high, step):
    def run(k, carry):
        step(k)
        return carry

    lax.fori_loop(low, high, run, 0)


def remote(src, dst, send_sem, recv_sem, chip, y, core):
    return pltpu.make_async_remote_copy(
        src_ref=src,
        dst_ref=dst,
        send_sem=send_sem,
        recv_sem=recv_sem,
        device_id={"seq": chip * 2 + core, "kvh": y},
        device_id_type=MESH,
    )


def with_ones(values):
    flipped = jnp.transpose(values.astype(F32))
    return jnp.concatenate([flipped, jnp.ones((16, values.shape[0]), F32)], axis=0).astype(BF16)


X_STEPS, Z_STEPS, Y_STEPS = (2, 1, 3, 0), (4, 3, 5, 2, 6, 1, 7, 0), (4, 3, 5, 2, 6, 1, 7, 0)
FAR_FIRST = [(dx, dz) for dx in X_STEPS for dz in Z_STEPS if dx or dz]


def join(peaks, parts):
    top = functools.reduce(jnp.maximum, peaks)
    total = None
    for peak, part in zip(peaks, parts):
        term = jnp.exp(peak - top) * part
        total = term if total is None else total + term
    stats = jnp.where(iota((8, 256), 0) == 1, top, total[128:136])
    return total[0:128], stats


def kernel(
    q_in,
    pk_in,
    pv_in,
    sk_in,
    sv_in,
    ck_in,
    cv_in,
    w_in,
    nk_ref,
    nv_ref,
    cont_prompt_ref,
    group_prompt_ref,
    prompt_len_ref,
    cont_len_ref,
    out_ref,
    q_line,
    keys,
    values,
    ck,
    cv,
    wt,
    parts,
    z_send,
    z_recv,
    att,
    att_f32,
    flat,
    y_send,
    y_recv,
    own_sem,
    w_ss,
    w_rs,
    kv_ss,
    kv_rs,
    fw_ss,
    fw_rs,
    col_sem,
    q_ss,
    q_rs,
    z_ss,
    z_rs,
    a_ss,
    a_rs,
    y_ss,
    y_rs,
):
    seq = lax.axis_index("seq")
    y = lax.axis_index("kvh")
    chip, c = seq // 2, seq % 2
    x, z = chip // NZ, chip % NZ
    other = 1 - c
    yc = y * 2 + c
    x_at = [lax.rem(x + d, NX) for d in range(NX)]
    x_to = [at * NZ for at in x_at]
    z_to = [lax.rem(z + d, NZ) for d in range(NZ)]
    y_to = [lax.rem(y + d, NY) for d in range(NY)]

    barrier = pltpu.get_barrier_semaphore()

    def greet(to_chip, to_y, to_c, sem=barrier):
        pl.semaphore_signal(
            sem, inc=1, device_id={"seq": to_chip * 2 + to_c, "kvh": to_y}, device_id_type=MESH
        )

    for dz in Z_STEPS[:-1]:
        greet(x_to[0] + z_to[dz], y, c)
    for dx in X_STEPS[:-1]:
        greet(x_to[dx] + z, y, c)
    for dy in (2, 6, 1, 7):
        greet(chip, y_to[dy], c)
        greet(chip, y_to[dy], other)
    greet(chip, y, other)

    local = [
        pltpu.make_async_copy(src, dst, own_sem.at[n])
        for n, (src, dst) in enumerate(
            [
                (q_in, q_line.at[z]),
                (pk_in, keys.at[x, c, pl.ds(0, 256)]),
                (sk_in, keys.at[x, c, pl.ds(256, 512)]),
                (pv_in, values.at[x, c, pl.ds(0, 256)]),
                (sv_in, values.at[x, c, pl.ds(256, 512)]),
                (ck_in, ck),
                (cv_in, cv),
                (w_in, wt.at[c, pl.ds(0, 80)]),
            ]
        )
    ]
    for copy in local:
        copy.start()
    for copy in local:
        copy.wait()
    pl.semaphore_wait(barrier, 19)

    def arrived(ref, sem):
        remote(ref, ref, q_ss, sem, chip, y, other).wait_recv()

    def left(ref, sem):
        remote(ref, ref, sem, q_rs, chip, y, other).wait_send()

    def kv_send(buffer, d, n, to):
        block = buffer.at[x_at[d], c]
        remote(block, block, kv_ss, kv_rs.at[n], x_to[to] + z, y, c).start()

    def to_core(buffer, d):
        block = buffer.at[x_at[d], c]
        remote(block, block, fw_ss, fw_rs.at[d], chip, y, other).start()

    kv_send(keys, 0, 0, 1)
    kv_send(values, 0, 1, 3)
    for dz in Z_STEPS[:-1]:
        block = q_line.at[z]
        remote(block, block, q_ss, q_rs, x_to[0] + z_to[dz], y, c).start()
    kv_send(values, 0, 2, 1)
    kv_send(keys, 0, 3, 3)
    to_core(keys, 0)
    to_core(values, 0)
    weights_swap = remote(
        wt.at[c, pl.ds(0, 80)], wt.at[c, pl.ds(0, 80)], w_ss, w_rs, chip, y, other
    )
    weights_swap.start()
    for dy in (2, 6):
        greet(chip, y_to[dy], c, col_sem)

    wt[:, 80:, :] = jnp.zeros((2, 48, wt.shape[2]), BF16)
    lane = iota((128, 256), 1)
    cont = (x * NZ + lane // ROWS) * 4 + c * 2 + (lane % ROWS) // 16
    widen = jnp.where(iota((128, 256), 0) == cont, 1.0, 0.0).astype(BF16)
    prompts = jnp.broadcast_to(cont_prompt_ref[...].astype(F32), (8, 128)).astype(BF16)
    prompt_of = dot(prompts, widen)[0:1]

    q_own = q_line[z]
    first = iota((ROWS, 1), 0) < 16
    past0 = dot_nt(q_own, ck[0]) * SCALING
    past1 = dot_nt(q_own, ck[1]) * SCALING
    lengths = jnp.where(first, cont_len_ref[0], cont_len_ref[1])
    past = jnp.where(iota(past0.shape, 1) < lengths, jnp.where(first, past0, past1), NEG)
    fresh_pad = jnp.zeros((12, HD), F32)
    nk = jnp.concatenate([nk_ref[0].astype(F32), nk_ref[1].astype(F32), fresh_pad], axis=0).astype(BF16)
    nv = jnp.concatenate([nv_ref[0].astype(F32), nv_ref[1].astype(F32), fresh_pad], axis=0).astype(BF16)
    fresh = dot_nt(q_own, nk) * SCALING
    row, col = iota(fresh.shape, 0), iota(fresh.shape, 1)
    seen = (col // 2 == row // 16) & (col % 2 <= (row // 8) % 2)
    fresh = jnp.where(seen, fresh, NEG)
    own_peak = jnp.maximum(jnp.max(past, axis=1, keepdims=True), jnp.max(fresh, axis=1, keepdims=True))
    past_w = jnp.exp(past - own_peak).astype(BF16)
    fresh_w = jnp.exp(fresh - own_peak).astype(BF16)
    own_total = jnp.sum(past_w.astype(F32), axis=1, keepdims=True) + jnp.sum(
        fresh_w.astype(F32), axis=1, keepdims=True
    )
    own_part = jnp.where(first, dot(past_w, cv[0]), dot(past_w, cv[1])) + dot(fresh_w, nv)
    def unit(n, at, core):
        prompt = group_prompt_ref[(at * NZ + z) // 2]
        length = prompt_len_ref[prompt]
        rows = q_line[...].reshape(NZ * ROWS, HD)
        scores = dot_nt(keys[at, core], rows) * SCALING
        flipped = with_ones(values[at, core])
        place = ((z % 2) * 2 + core) * 512 + iota((512, 1), 0)
        store = jnp.where(place < length, scores[256:], NEG)
        prefix_peak = jnp.max(scores[:256], axis=0, keepdims=True)
        store_peak = jnp.max(store, axis=0, keepdims=True)
        prefix = dot(flipped[:, :256], jnp.exp(scores[:256] - prefix_peak).astype(BF16))
        store = dot(flipped[:, 256:], jnp.exp(store - store_peak).astype(BF16))
        mine = prompt_of == jnp.full((1, 256), prompt, jnp.int32).astype(F32)
        part, stats = join([prefix_peak, jnp.where(mine, store_peak, NEG)], [prefix[0:136], store[0:136]])
        parts[n, 0:128] = part
        parts[n, 128:136] = stats

    def from_core(d):
        arrived(keys.at[0], fw_rs.at[d])

    arrived(keys.at[0, 0], kv_rs.at[0])
    kv_send(keys, 3, 4, 1)
    to_core(keys, 3)
    arrived(keys.at[0, 0], kv_rs.at[1])
    kv_send(values, 1, 5, 3)
    to_core(values, 1)
    arrived(q_line.at[pl.ds(0, NZ - 1)], q_rs)
    unit(0, x, c)
    from_core(0)
    unit(1, x, other)
    arrived(keys.at[0, 0], kv_rs.at[2])
    to_core(values, 3)
    arrived(keys.at[0, 0], kv_rs.at[3])
    to_core(keys, 1)
    loop(0, 2, lambda i: unit(2 + i, lax.rem(x + 3 - 2 * i, NX), c))
    from_core(3)
    from_core(1)
    loop(0, 2, lambda i: unit(4 + i, lax.rem(x + 3 - 2 * i, NX), other))
    arrived(keys.at[0, 0], kv_rs.at[4])
    to_core(keys, 2)
    arrived(keys.at[0, 0], kv_rs.at[5])
    to_core(values, 2)
    unit(6, x_at[2], c)
    from_core(2)
    unit(7, x_at[2], other)
    part, stats = join([parts[n, 129:130] for n in range(8)], [parts[n] for n in range(8)])

    by_row = jnp.transpose(part)
    for t in range(NZ):
        half = stats[:, (t // 4) * 128 : (t // 4 + 1) * 128]
        turned = half if t % 4 == 0 else pltpu.roll(half, 128 - (t % 4) * ROWS, 1)
        z_send[t, 0:ROWS] = by_row[t * ROWS : (t + 1) * ROWS]
        z_send[t, ROWS : ROWS + 8] = turned

    for dz in Z_STEPS[:-1]:
        to = z_to[dz]
        remote(z_send.at[to], z_recv.at[z], z_ss, z_rs, x_to[0] + to, y, c).start()
    z_recv[z] = z_send[z]
    left(q_line.at[pl.ds(0, NZ - 1)], q_ss)
    left(keys.at[pl.ds(0, 3)], kv_ss)
    left(keys, fw_ss)
    weights_swap.wait()
    pl.semaphore_wait(col_sem, 2)
    arrived(z_recv.at[pl.ds(0, NZ - 1)], z_rs)

    side = jnp.concatenate(
        [z_recv[s, ROWS + 1 : ROWS + 2] for s in range(NZ)]
        + [z_recv[s, ROWS : ROWS + 1] for s in range(NZ)]
        + [jnp.zeros((112, 128), F32)],
        axis=0,
    )
    side = jnp.transpose(side)[0:ROWS]
    top = jnp.maximum(jnp.max(side[:, 0:NZ], axis=1, keepdims=True), own_peak)
    own_factor = jnp.exp(own_peak - top)
    total, weighted = own_factor * own_total, own_factor * own_part
    for s in range(NZ):
        factor = jnp.exp(side[:, s : s + 1] - top)
        total = total + factor * side[:, NZ + s : NZ + s + 1]
        weighted = weighted + factor * z_recv[s, 0:ROWS]
    att[chip] = (weighted / total).astype(BF16)

    for dx, dz in FAR_FIRST:
        block = att.at[chip]
        remote(block, block, a_ss, a_rs, x_to[dx] + z_to[dz], y, c).start()
    left(z_send.at[pl.ds(0, NZ - 1)], z_ss)
    arrived(att.at[pl.ds(0, CHIPS - 1)], a_rs)

    att_f32[...] = att[...].reshape(CHIPS * ROWS, HD).astype(F32)
    for h in range(GROUP):
        flat[:, h * HD : (h + 1) * HD] = att_f32[pl.ds(h, 128, stride=GROUP), :].astype(BF16)
    for b in range(2):
        y_send[b] = dot_nt(flat[...], wt[b]).reshape(NY, 16, 128)
    for dy in Y_STEPS:
        for dc in (1, 0):
            if dy or dc:
                to_y, to_c = y_to[dy], other if dc else c
                remote(y_send.at[to_c, to_y], y_recv.at[yc], y_ss, y_rs, chip, to_y, to_c).start()
    y_recv[yc] = y_send[c, y]
    left(att.at[pl.ds(0, CHIPS - 1)], a_ss)
    arrived(y_recv.at[pl.ds(0, 15)], y_rs)
    for b in range(2):
        summed = functools.reduce(jnp.add, [y_recv[n * 2 + b] for n in range(NY)])
        for n in range(4):
            for i in range(2):
                out_ref[n * 4 + b * 2 + i] = summed[n * 4 + i * 2 : n * 4 + i * 2 + 2, 0:80]

    left(y_recv.at[pl.ds(0, 15)], y_ss)


def body(
    queries,
    new_keys,
    new_values,
    prefix_keys,
    prefix_values,
    prompt_keys,
    prompt_values,
    cache_keys,
    cache_values,
    group_prompt,
    prompt_len,
    cont_prompt,
    cont_len,
    out_weight,
):
    anywhere = pl.BlockSpec(memory_space=pl.ANY)
    vmem = pl.BlockSpec(memory_space=pltpu.VMEM)
    smem = pl.BlockSpec(memory_space=pltpu.SMEM)
    dma = pltpu.SemaphoreType.DMA
    return pl.pallas_call(
        kernel,
        out_shape=jax.ShapeDtypeStruct((16, 2, 80), F32),
        in_specs=[anywhere] * 8 + [vmem] * 3 + [smem] * 3,
        out_specs=vmem,
        scratch_shapes=[
            pltpu.VMEM((NZ, ROWS, HD), BF16),
            pltpu.VMEM((NX, 2, 768, HD), BF16),
            pltpu.VMEM((NX, 2, 768, HD), BF16),
            pltpu.VMEM((2, 256, HD), BF16),
            pltpu.VMEM((2, 256, HD), BF16),
            pltpu.VMEM((2, 128, 1024), BF16),
            pltpu.VMEM((8, 136, 256), F32),
            pltpu.VMEM((NZ, 40, 128), F32),
            pltpu.VMEM((NZ, 40, 128), F32),
            pltpu.VMEM((CHIPS, ROWS, HD), BF16),
            pltpu.VMEM((CHIPS * ROWS, HD), F32),
            pltpu.VMEM((128, 1024), BF16),
            pltpu.VMEM((2, NY, 16, 128), F32),
            pltpu.VMEM((16, 16, 128), F32),
            dma((8,)),
            dma,
            dma,
            dma,
            dma((6,)),
            dma,
            dma((NX,)),
            pltpu.SemaphoreType.REGULAR,
            dma,
            dma,
            dma,
            dma,
            dma,
            dma,
            dma,
            dma,
        ],
        compiler_params=pltpu.CompilerParams(
            collective_id=0, has_side_effects=True, vmem_limit_bytes=55168 << 10
        ),
    )(
        queries.reshape(ROWS, HD),
        prefix_keys[:, 0, :],
        prefix_values[:, 0, :],
        prompt_keys[:, 0, :],
        prompt_values[:, 0, :],
        cache_keys[:, :, 0, :],
        cache_values[:, :, 0, :],
        out_weight.T,
        new_keys[:, :, 0, :],
        new_values[:, :, 0, :],
        cont_prompt.reshape(1, 128),
        group_prompt,
        prompt_len,
        cont_len,
    )


def solution(mesh):
    in_specs = (
        P("seq", None, "kvh", None),
        P("seq", None, "kvh", None),
        P("seq", None, "kvh", None),
        P("seq", "kvh", None),
        P("seq", "kvh", None),
        P("seq", "kvh", None),
        P("seq", "kvh", None),
        P("seq", None, "kvh", None),
        P("seq", None, "kvh", None),
        P(),
        P(),
        P(),
        P("seq"),
        P("kvh", "seq"),
    )
    out_specs = P("kvh", None, "seq")
    return jax.shard_map(body, mesh=mesh, in_specs=in_specs, out_specs=out_specs, check_vma=False)
```

```python
import functools
import math

import jax
import jax.numpy as jnp
from jax import lax
from jax.experimental import pallas as pl
from jax.experimental.pallas import tpu as pltpu
from jax.sharding import PartitionSpec as P

NEG = -1e30
MESH = pl.DeviceIdType.MESH
F32, BF16 = jnp.float32, jnp.bfloat16
NX, NZ, NC, NY = 4, 8, 2, 8
CHIPS = NX * NZ
ROWS = 32
HD = 128
GROUP = 8
SCALING = 1.0 / math.sqrt(HD)


def dot(a, b):
    return jnp.dot(a, b, preferred_element_type=F32)


def dot_nt(a, b):
    return lax.dot_general(a, b, (((1,), (1,)), ((), ())), preferred_element_type=F32)


def iota(shape, axis):
    return lax.broadcasted_iota(jnp.int32, shape, axis)


def loop(low, high, step):
    def run(k, carry):
        step(k)
        return carry

    lax.fori_loop(low, high, run, 0)


def remote(src, dst, send_sem, recv_sem, chip, y, core):
    return pltpu.make_async_remote_copy(
        src_ref=src,
        dst_ref=dst,
        send_sem=send_sem,
        recv_sem=recv_sem,
        device_id={"seq": chip * 2 + core, "kvh": y},
        device_id_type=MESH,
    )


def with_ones(values):
    flipped = jnp.transpose(values.astype(F32))
    return jnp.concatenate([flipped, jnp.ones((16, values.shape[0]), F32)], axis=0).astype(BF16)


X_STEPS, Z_STEPS, Y_STEPS = (2, 1, 3, 0), (4, 3, 5, 2, 6, 1, 7, 0), (4, 3, 5, 2, 6, 1, 7, 0)
FAR_FIRST = [(dx, dz) for dx in X_STEPS for dz in Z_STEPS if dx or dz]


def join(peaks, parts):
    top = functools.reduce(jnp.maximum, peaks)
    total = None
    for peak, part in zip(peaks, parts):
        term = jnp.exp(peak - top) * part
        total = term if total is None else total + term
    stats = jnp.where(iota((8, 256), 0) == 1, top, total[128:136])
    return total[0:128], stats


def kernel(
    q_in,
    pk_in,
    pv_in,
    sk_in,
    sv_in,
    ck_in,
    cv_in,
    w_in,
    nk_ref,
    nv_ref,
    cont_prompt_ref,
    group_prompt_ref,
    prompt_len_ref,
    cont_len_ref,
    out_ref,
    q_line,
    keys,
    values,
    ck,
    cv,
    wt,
    parts,
    z_send,
    z_recv,
    att,
    att_f32,
    flat,
    y_send,
    y_recv,
    own_sem,
    w_ss,
    w_rs,
    kv_ss,
    kv_rs,
    fw_ss,
    fw_rs,
    col_sem,
    q_ss,
    q_rs,
    z_ss,
    z_rs,
    a_ss,
    a_rs,
    y_ss,
    y_rs,
):
    seq = lax.axis_index("seq")
    y = lax.axis_index("kvh")
    chip, c = seq // 2, seq % 2
    x, z = chip // NZ, chip % NZ
    other = 1 - c
    yc = y * 2 + c
    x_at = [lax.rem(x + d, NX) for d in range(NX)]
    x_to = [at * NZ for at in x_at]
    z_to = [lax.rem(z + d, NZ) for d in range(NZ)]
    y_to = [lax.rem(y + d, NY) for d in range(NY)]

    barrier = pltpu.get_barrier_semaphore()

    def greet(to_chip, to_y, to_c, sem=barrier):
        pl.semaphore_signal(
            sem, inc=1, device_id={"seq": to_chip * 2 + to_c, "kvh": to_y}, device_id_type=MESH
        )

    for dx in (1, 3):
        greet(x_to[dx] + z, y, c)
    for dz in (2, 6, 1, 7):
        greet(x_to[0] + z_to[dz], y, c)
    for dy in (2, 6, 1, 7):
        greet(chip, y_to[dy], c)
        greet(chip, y_to[dy], other)
    greet(chip, y, other)

    local = [
        pltpu.make_async_copy(src, dst, own_sem.at[n])
        for n, (src, dst) in enumerate(
            [
                (q_in, q_line.at[z]),
                (pk_in, keys.at[x, c, pl.ds(0, 256)]),
                (sk_in, keys.at[x, c, pl.ds(256, 512)]),
                (pv_in, values.at[x, c, pl.ds(0, 256)]),
                (sv_in, values.at[x, c, pl.ds(256, 512)]),
                (ck_in, ck),
                (cv_in, cv),
                (w_in, wt.at[c, pl.ds(0, 80)]),
            ]
        )
    ]
    for copy in local:
        copy.start()
    pl.semaphore_wait(barrier, 15)

    def arrived(ref, sem):
        remote(ref, ref, q_ss, sem, chip, y, other).wait_recv()

    def left(ref, sem):
        remote(ref, ref, sem, q_rs.at[0], chip, y, other).wait_send()

    def own_to_x(prefix, store, buffer, n, to):
        for src, first, count in ((store, 256, 512), (prefix, 0, 256)):
            dst = buffer.at[x, c, pl.ds(first, count)]
            remote(src, dst, kv_ss, kv_rs.at[n], x_to[to] + z, y, c).start()

    def relay(buffer, d, n, to):
        block = buffer.at[x_at[d], c]
        remote(block, block, kv_ss, kv_rs.at[n], x_to[to] + z, y, c).start()

    def to_core(buffer, d):
        block = buffer.at[x_at[d], c]
        remote(block, block, fw_ss, fw_rs.at[d], chip, y, other).start()

    def q_send(dz, n, to):
        block = q_line.at[z_to[dz]]
        src = block if dz else q_in
        remote(src, block, q_ss, q_rs.at[n], x_to[0] + z_to[to], y, c).start()

    own_to_x(pk_in, sk_in, keys, 0, 1)
    own_to_x(pv_in, sv_in, values, 1, 3)
    for dz in (2, 6, 1, 7):
        q_send(0, 0, dz)
    own_to_x(pv_in, sv_in, values, 2, 1)
    own_to_x(pk_in, sk_in, keys, 3, 3)
    for copy in local:
        copy.wait()
    to_core(keys, 0)
    to_core(values, 0)
    weights_swap = remote(
        wt.at[c, pl.ds(0, 80)], wt.at[c, pl.ds(0, 80)], w_ss, w_rs, chip, y, other
    )
    weights_swap.start()
    for dy in (2, 6):
        greet(chip, y_to[dy], c, col_sem)

    wt[:, 80:, :] = jnp.zeros((2, 48, wt.shape[2]), BF16)
    lane = iota((128, 256), 1)
    cont = (x * NZ + lane // ROWS) * 4 + c * 2 + (lane % ROWS) // 16
    widen = jnp.where(iota((128, 256), 0) == cont, 1.0, 0.0).astype(BF16)
    prompts = jnp.broadcast_to(cont_prompt_ref[...].astype(F32), (8, 128)).astype(BF16)
    prompt_of = dot(prompts, widen)[0:1]

    q_own = q_line[z]
    first = iota((ROWS, 1), 0) < 16
    past0 = dot_nt(q_own, ck[0]) * SCALING
    past1 = dot_nt(q_own, ck[1]) * SCALING
    lengths = jnp.where(first, cont_len_ref[0], cont_len_ref[1])
    past = jnp.where(iota(past0.shape, 1) < lengths, jnp.where(first, past0, past1), NEG)
    fresh_pad = jnp.zeros((12, HD), F32)
    nk = jnp.concatenate([nk_ref[0].astype(F32), nk_ref[1].astype(F32), fresh_pad], axis=0).astype(BF16)
    nv = jnp.concatenate([nv_ref[0].astype(F32), nv_ref[1].astype(F32), fresh_pad], axis=0).astype(BF16)
    fresh = dot_nt(q_own, nk) * SCALING
    row, col = iota(fresh.shape, 0), iota(fresh.shape, 1)
    seen = (col // 2 == row // 16) & (col % 2 <= (row // 8) % 2)
    fresh = jnp.where(seen, fresh, NEG)
    own_peak = jnp.maximum(jnp.max(past, axis=1, keepdims=True), jnp.max(fresh, axis=1, keepdims=True))
    past_w = jnp.exp(past - own_peak).astype(BF16)
    fresh_w = jnp.exp(fresh - own_peak).astype(BF16)
    own_total = jnp.sum(past_w.astype(F32), axis=1, keepdims=True) + jnp.sum(
        fresh_w.astype(F32), axis=1, keepdims=True
    )
    own_part = jnp.where(first, dot(past_w, cv[0]), dot(past_w, cv[1])) + dot(fresh_w, nv)
    def unit(n, at, core):
        prompt = group_prompt_ref[(at * NZ + z) // 2]
        length = prompt_len_ref[prompt]
        rows = q_line[...].reshape(NZ * ROWS, HD)
        scores = dot_nt(keys[at, core], rows) * SCALING
        flipped = with_ones(values[at, core])
        place = ((z % 2) * 2 + core) * 512 + iota((512, 1), 0)
        store = jnp.where(place < length, scores[256:], NEG)
        prefix_peak = jnp.max(scores[:256], axis=0, keepdims=True)
        store_peak = jnp.max(store, axis=0, keepdims=True)
        prefix = dot(flipped[:, :256], jnp.exp(scores[:256] - prefix_peak).astype(BF16))
        store = dot(flipped[:, 256:], jnp.exp(store - store_peak).astype(BF16))
        mine = prompt_of == jnp.full((1, 256), prompt, jnp.int32).astype(F32)
        part, stats = join([prefix_peak, jnp.where(mine, store_peak, NEG)], [prefix[0:136], store[0:136]])
        parts[n, 0:128] = part
        parts[n, 128:136] = stats

    def from_core(d):
        arrived(keys.at[0], fw_rs.at[d])

    arrived(q_line.at[pl.ds(0, 4)], q_rs.at[0])
    q_send(1, 1, 6)
    q_send(2, 1, 6)
    q_send(7, 1, 2)
    arrived(keys.at[0, 0], kv_rs.at[0])
    relay(keys, 3, 4, 1)
    to_core(keys, 3)
    arrived(keys.at[0, 0], kv_rs.at[1])
    relay(values, 1, 5, 3)
    to_core(values, 1)
    arrived(q_line.at[pl.ds(0, 3)], q_rs.at[1])
    unit(0, x, c)
    from_core(0)
    unit(1, x, other)
    arrived(keys.at[0, 0], kv_rs.at[2])
    to_core(values, 3)
    arrived(keys.at[0, 0], kv_rs.at[3])
    to_core(keys, 1)
    loop(0, 2, lambda i: unit(2 + i, lax.rem(x + 3 - 2 * i, NX), c))
    from_core(3)
    from_core(1)
    loop(0, 2, lambda i: unit(4 + i, lax.rem(x + 3 - 2 * i, NX), other))
    arrived(keys.at[0, 0], kv_rs.at[4])
    to_core(keys, 2)
    arrived(keys.at[0, 0], kv_rs.at[5])
    to_core(values, 2)
    unit(6, x_at[2], c)
    from_core(2)
    unit(7, x_at[2], other)
    part, stats = join([parts[n, 129:130] for n in range(8)], [parts[n] for n in range(8)])

    by_row = jnp.transpose(part)
    for t in range(NZ):
        half = stats[:, (t // 4) * 128 : (t // 4 + 1) * 128]
        turned = half if t % 4 == 0 else pltpu.roll(half, 128 - (t % 4) * ROWS, 1)
        z_send[t, 0:ROWS] = by_row[t * ROWS : (t + 1) * ROWS]
        z_send[t, ROWS : ROWS + 2] = turned[0:2]

    for dz in Z_STEPS[:-1]:
        to = z_to[dz]
        remote(z_send.at[to], z_recv.at[z], z_ss, z_rs, x_to[0] + to, y, c).start()
    z_recv[z] = z_send[z]
    left(q_line.at[pl.ds(0, NZ - 1)], q_ss)
    left(keys.at[pl.ds(0, 3)], kv_ss)
    left(keys, fw_ss)
    weights_swap.wait()
    pl.semaphore_wait(col_sem, 2)
    arrived(z_recv.at[pl.ds(0, NZ - 1)], z_rs)

    side = jnp.concatenate(
        [z_recv[s, ROWS + 1 : ROWS + 2] for s in range(NZ)]
        + [z_recv[s, ROWS : ROWS + 1] for s in range(NZ)]
        + [jnp.zeros((112, 128), F32)],
        axis=0,
    )
    side = jnp.transpose(side)[0:ROWS]
    top = jnp.maximum(jnp.max(side[:, 0:NZ], axis=1, keepdims=True), own_peak)
    own_factor = jnp.exp(own_peak - top)
    total, weighted = own_factor * own_total, own_factor * own_part
    for s in range(NZ):
        factor = jnp.exp(side[:, s : s + 1] - top)
        total = total + factor * side[:, NZ + s : NZ + s + 1]
        weighted = weighted + factor * z_recv[s, 0:ROWS]
    att[chip] = (weighted / total).astype(BF16)

    for dx, dz in FAR_FIRST:
        block = att.at[chip]
        remote(block, block, a_ss, a_rs, x_to[dx] + z_to[dz], y, c).start()
    left(z_send.at[pl.ds(0, NZ - 1)], z_ss)
    arrived(att.at[pl.ds(0, CHIPS - 1)], a_rs)

    att_f32[...] = att[...].reshape(CHIPS * ROWS, HD).astype(F32)
    for h in range(GROUP):
        flat[:, h * HD : (h + 1) * HD] = att_f32[pl.ds(h, 128, stride=GROUP), :].astype(BF16)
    for to_c in (other, c):
        y_send[to_c] = dot_nt(flat[...], wt[to_c]).reshape(NY, 16, 128)
        for dy in Y_STEPS if to_c is other else Y_STEPS[:-1]:
            to_y = y_to[dy]
            remote(y_send.at[to_c, to_y], y_recv.at[yc], y_ss, y_rs, chip, to_y, to_c).start()
    y_recv[yc] = y_send[c, y]
    left(att.at[pl.ds(0, CHIPS - 1)], a_ss)
    arrived(y_recv.at[pl.ds(0, 15)], y_rs)
    for b in range(2):
        summed = functools.reduce(jnp.add, [y_recv[n * 2 + b] for n in range(NY)])
        for n in range(4):
            for i in range(2):
                out_ref[n * 4 + b * 2 + i] = summed[n * 4 + i * 2 : n * 4 + i * 2 + 2, 0:80]

    left(y_recv.at[pl.ds(0, 15)], y_ss)


def body(
    queries,
    new_keys,
    new_values,
    prefix_keys,
    prefix_values,
    prompt_keys,
    prompt_values,
    cache_keys,
    cache_values,
    group_prompt,
    prompt_len,
    cont_prompt,
    cont_len,
    out_weight,
):
    anywhere = pl.BlockSpec(memory_space=pl.ANY)
    vmem = pl.BlockSpec(memory_space=pltpu.VMEM)
    smem = pl.BlockSpec(memory_space=pltpu.SMEM)
    dma = pltpu.SemaphoreType.DMA
    return pl.pallas_call(
        kernel,
        out_shape=jax.ShapeDtypeStruct((16, 2, 80), F32),
        in_specs=[anywhere] * 8 + [vmem] * 3 + [smem] * 3,
        out_specs=vmem,
        scratch_shapes=[
            pltpu.VMEM((NZ, ROWS, HD), BF16),
            pltpu.VMEM((NX, 2, 768, HD), BF16),
            pltpu.VMEM((NX, 2, 768, HD), BF16),
            pltpu.VMEM((2, 256, HD), BF16),
            pltpu.VMEM((2, 256, HD), BF16),
            pltpu.VMEM((2, 128, 1024), BF16),
            pltpu.VMEM((8, 136, 256), F32),
            pltpu.VMEM((NZ, 34, 128), F32),
            pltpu.VMEM((NZ, 34, 128), F32),
            pltpu.VMEM((CHIPS, ROWS, HD), BF16),
            pltpu.VMEM((CHIPS * ROWS, HD), F32),
            pltpu.VMEM((128, 1024), BF16),
            pltpu.VMEM((2, NY, 16, 128), F32),
            pltpu.VMEM((16, 16, 128), F32),
            dma((8,)),
            dma,
            dma,
            dma,
            dma((6,)),
            dma,
            dma((NX,)),
            pltpu.SemaphoreType.REGULAR,
            dma,
            dma((2,)),
            dma,
            dma,
            dma,
            dma,
            dma,
            dma,
        ],
        compiler_params=pltpu.CompilerParams(
            collective_id=0, has_side_effects=True, vmem_limit_bytes=55168 << 10
        ),
    )(
        queries.reshape(ROWS, HD),
        prefix_keys[:, 0, :],
        prefix_values[:, 0, :],
        prompt_keys[:, 0, :],
        prompt_values[:, 0, :],
        cache_keys[:, :, 0, :],
        cache_values[:, :, 0, :],
        out_weight.T,
        new_keys[:, :, 0, :],
        new_values[:, :, 0, :],
        cont_prompt.reshape(1, 128),
        group_prompt,
        prompt_len,
        cont_len,
    )


def solution(mesh):
    in_specs = (
        P("seq", None, "kvh", None),
        P("seq", None, "kvh", None),
        P("seq", None, "kvh", None),
        P("seq", "kvh", None),
        P("seq", "kvh", None),
        P("seq", "kvh", None),
        P("seq", "kvh", None),
        P("seq", None, "kvh", None),
        P("seq", None, "kvh", None),
        P(),
        P(),
        P(),
        P("seq"),
        P("kvh", "seq"),
    )
    out_specs = P("kvh", None, "seq")
    return jax.shard_map(body, mesh=mesh, in_specs=in_specs, out_specs=out_specs, check_vma=False)
```

```python
import functools
import math

import jax
import jax.numpy as jnp
from jax import lax
from jax.experimental import pallas as pl
from jax.experimental.pallas import tpu as pltpu
from jax.sharding import PartitionSpec as P

NEG = -1e30
MESH = pl.DeviceIdType.MESH
F32, BF16 = jnp.float32, jnp.bfloat16
NX, NZ, NC, NY = 4, 8, 2, 8
CHIPS = NX * NZ
ROWS = 32
HD = 128
GROUP = 8
SCALING = 1.0 / math.sqrt(HD)


def dot(a, b):
    return jnp.dot(a, b, preferred_element_type=F32)


def dot_nt(a, b):
    return lax.dot_general(a, b, (((1,), (1,)), ((), ())), preferred_element_type=F32)


def iota(shape, axis):
    return lax.broadcasted_iota(jnp.int32, shape, axis)


def loop(low, high, step):
    def run(k, carry):
        step(k)
        return carry

    lax.fori_loop(low, high, run, 0)


def remote(src, dst, send_sem, recv_sem, chip, y, core):
    return pltpu.make_async_remote_copy(
        src_ref=src,
        dst_ref=dst,
        send_sem=send_sem,
        recv_sem=recv_sem,
        device_id={"seq": chip * 2 + core, "kvh": y},
        device_id_type=MESH,
    )


def with_ones(values):
    flipped = jnp.transpose(values.astype(F32))
    return jnp.concatenate([flipped, jnp.ones((16, values.shape[0]), F32)], axis=0).astype(BF16)


X_STEPS, Z_STEPS, Y_STEPS = (2, 1, 3, 0), (4, 3, 5, 2, 6, 1, 7, 0), (4, 3, 5, 2, 6, 1, 7, 0)
FAR_FIRST = [(dx, dz) for dx in X_STEPS for dz in Z_STEPS if dx or dz]


def join(peaks, parts):
    top = functools.reduce(jnp.maximum, peaks)
    total = None
    for peak, part in zip(peaks, parts):
        term = jnp.exp(peak - top) * part
        total = term if total is None else total + term
    stats = jnp.where(iota((8, 256), 0) == 1, top, total[128:136])
    return total[0:128], stats


def kernel(
    q_in,
    pk_in,
    pv_in,
    sk_in,
    sv_in,
    ck_in,
    cv_in,
    w_in,
    nk_ref,
    nv_ref,
    cont_prompt_ref,
    group_prompt_in,
    prompt_len_in,
    cont_len_in,
    out_ref,
    group_prompt_ref,
    prompt_len_ref,
    cont_len_ref,
    q_line,
    q_other,
    keys,
    values,
    ck,
    cv,
    wt,
    parts,
    p_send,
    p_recv,
    z_send,
    z_recv,
    att,
    att_f32,
    flat,
    y_send,
    y_recv,
    own_sem,
    w_ss,
    w_rs,
    kv_ss,
    kv_rs,
    swap_ss,
    swap_rs,
    col_sem,
    q_ss,
    q_rs,
    z_ss,
    z_rs,
    a_ss,
    a_rs,
    y_ss,
    y_rs,
):
    seq = lax.axis_index("seq")
    y = lax.axis_index("kvh")
    chip, c = seq // 2, seq % 2
    x, z = chip // NZ, chip % NZ
    other = 1 - c
    yc = y * 2 + c
    x_at = [lax.rem(x + d, NX) for d in range(NX)]
    x_to = [at * NZ for at in x_at]
    z_to = [lax.rem(z + d, NZ) for d in range(NZ)]
    y_to = [lax.rem(y + d, NY) for d in range(NY)]

    barrier = pltpu.get_barrier_semaphore()

    def greet(to_chip, to_y, to_c, sem=barrier):
        pl.semaphore_signal(
            sem, inc=1, device_id={"seq": to_chip * 2 + to_c, "kvh": to_y}, device_id_type=MESH
        )

    for dx in (1, 3):
        greet(x_to[dx] + z, y, c)
    for dz in (2, 6, 1, 7):
        greet(x_to[0] + z_to[dz], y, c)
    for dy in (2, 6, 1, 7):
        greet(chip, y_to[dy], c)
        greet(chip, y_to[dy], other)
    greet(chip, y, other)

    local = [
        pltpu.make_async_copy(src, dst, own_sem.at[n])
        for n, (src, dst) in enumerate(
            [
                (q_in, q_line.at[z]),
                (pk_in, keys.at[x, pl.ds(0, 256)]),
                (sk_in, keys.at[x, pl.ds(256, 512)]),
                (pv_in, values.at[x, pl.ds(0, 256)]),
                (sv_in, values.at[x, pl.ds(256, 512)]),
                (ck_in, ck),
                (cv_in, cv),
                (w_in, wt.at[c, pl.ds(0, 80)]),
                (group_prompt_in, group_prompt_ref),
                (prompt_len_in, prompt_len_ref),
                (cont_len_in, cont_len_ref),
            ]
        )
    ]
    for copy in local:
        copy.start()
    pl.semaphore_wait(barrier, 15)

    def arrived(ref, sem):
        remote(ref, ref, q_ss, sem, chip, y, other).wait_recv()

    def left(ref, sem):
        remote(ref, ref, sem, q_rs.at[0], chip, y, other).wait_send()

    def own_to_x(prefix, store, buffer, n, to):
        for src, start, count in ((store, 256, 512), (prefix, 0, 256)):
            dst = buffer.at[x, pl.ds(start, count)]
            remote(src, dst, kv_ss.at[n % 2], kv_rs.at[n], x_to[to] + z, y, c).start()

    def relay(buffer, d, n, to):
        for m, start, count in ((n, 256, 512), (n + 2, 0, 256)):
            block = buffer.at[x_at[d], pl.ds(start, count)]
            remote(block, block, kv_ss.at[n % 2], kv_rs.at[m], x_to[to] + z, y, c).start()

    def swap(src, dst, n):
        return remote(src, dst, swap_ss.at[n], swap_rs.at[n], chip, y, other)

    def q_send(dz, n, to):
        block = q_line.at[z_to[dz]]
        src = block if dz else q_in
        remote(src, block, q_ss, q_rs.at[n], x_to[0] + z_to[to], y, c).start()

    own_to_x(pk_in, sk_in, keys, 0, 1)
    own_to_x(pv_in, sv_in, values, 1, 3)
    for dz in (2, 6, 1, 7):
        q_send(0, 0, dz)
    own_to_x(pv_in, sv_in, values, 3, 1)
    own_to_x(pk_in, sk_in, keys, 2, 3)
    for copy in local:
        copy.wait()
    weights_swap = remote(
        wt.at[c, pl.ds(0, 80)], wt.at[c, pl.ds(0, 80)], w_ss, w_rs, chip, y, other
    )
    weights_swap.start()
    for dy in (2, 6):
        greet(chip, y_to[dy], c, col_sem)

    wt[:, 80:, :] = jnp.zeros((2, 48, wt.shape[2]), BF16)
    lane = iota((128, 256), 1)
    prompts = jnp.broadcast_to(cont_prompt_ref[...].astype(F32), (8, 128)).astype(BF16)
    prompt_of = []
    for core in (c, other):
        cont = (x * NZ + lane // ROWS) * 4 + core * 2 + (lane % ROWS) // 16
        widen = jnp.where(iota((128, 256), 0) == cont, 1.0, 0.0).astype(BF16)
        prompt_of.append(dot(prompts, widen)[0:1])

    q_own = q_line[z]
    first = iota((ROWS, 1), 0) < 16
    past0 = dot_nt(q_own, ck[0]) * SCALING
    past1 = dot_nt(q_own, ck[1]) * SCALING
    lengths = jnp.where(first, cont_len_ref[0], cont_len_ref[1])
    past = jnp.where(iota(past0.shape, 1) < lengths, jnp.where(first, past0, past1), NEG)
    fresh_pad = jnp.zeros((12, HD), F32)
    nk = jnp.concatenate([nk_ref[0].astype(F32), nk_ref[1].astype(F32), fresh_pad], axis=0).astype(BF16)
    nv = jnp.concatenate([nv_ref[0].astype(F32), nv_ref[1].astype(F32), fresh_pad], axis=0).astype(BF16)
    fresh = dot_nt(q_own, nk) * SCALING
    row, col = iota(fresh.shape, 0), iota(fresh.shape, 1)
    seen = (col // 2 == row // 16) & (col % 2 <= (row // 8) % 2)
    fresh = jnp.where(seen, fresh, NEG)
    own_peak = jnp.maximum(jnp.max(past, axis=1, keepdims=True), jnp.max(fresh, axis=1, keepdims=True))
    past_w = jnp.exp(past - own_peak).astype(BF16)
    fresh_w = jnp.exp(fresh - own_peak).astype(BF16)
    own_total = jnp.sum(past_w.astype(F32), axis=1, keepdims=True) + jnp.sum(
        fresh_w.astype(F32), axis=1, keepdims=True
    )
    own_part = jnp.where(first, dot(past_w, cv[0]), dot(past_w, cv[1])) + dot(fresh_w, nv)
    def rows_of(r):
        return (q_other if r else q_line)[...].reshape(NZ * ROWS, HD)

    def prefix_block(at, flipped, r):
        scores = dot_nt(keys[at, 0:256], rows_of(r)) * SCALING
        peak = jnp.max(scores, axis=0, keepdims=True)
        return peak, dot(flipped, jnp.exp(scores - peak).astype(BF16))[0:136]

    def store_block(at, flipped, r):
        prompt = group_prompt_ref[(at * NZ + z) // 2]
        place = ((z % 2) * 2 + c) * 512 + iota((512, 1), 0)
        scores = dot_nt(keys[at, 256:768], rows_of(r)) * SCALING
        scores = jnp.where(place < prompt_len_ref[prompt], scores, NEG)
        peak = jnp.max(scores, axis=0, keepdims=True)
        part = dot(flipped, jnp.exp(scores - peak).astype(BF16))[0:136]
        mine = prompt_of[r] == jnp.full((1, 256), prompt, jnp.int32).astype(F32)
        return jnp.where(mine, peak, NEG), part

    def keep(ref, part, stats):
        ref[0:128] = part
        ref[128:136] = stats

    def unit(n, at, row_sets):
        flipped = with_ones(values[at])
        for r in row_sets:
            blocks = [prefix_block(at, flipped[:, :256], r), store_block(at, flipped[:, 256:], r)]
            keep(parts.at[r, n], *join(*zip(*blocks)))

    def joined(r, more):
        kept = [(parts[r, n, 129:130], parts[r, n]) for n in range(4)]
        return join(*zip(*(kept + more)))

    arrived(q_line.at[pl.ds(0, 4)], q_rs.at[0])
    q_send(1, 1, 6)
    q_send(2, 1, 6)
    q_send(7, 1, 2)
    arrived(keys.at[0], kv_rs.at[0])
    relay(keys, 3, 4, 1)
    arrived(keys.at[0], kv_rs.at[1])
    relay(values, 1, 5, 3)
    arrived(q_line.at[pl.ds(0, 3)], q_rs.at[1])
    q_swap = swap(q_line, q_other, 0)
    q_swap.start()
    unit(0, x, (0,))
    q_swap.wait_recv()
    unit(0, x, (1,))
    arrived(keys.at[0], kv_rs.at[2])
    arrived(keys.at[0], kv_rs.at[3])
    loop(0, 2, lambda i: unit(1 + i, lax.rem(x + 3 - 2 * i, NX), (0, 1)))
    far = x_at[2]
    arrived(keys.at[0, pl.ds(256, 512)], kv_rs.at[4])
    arrived(keys.at[0, pl.ds(256, 512)], kv_rs.at[5])
    flipped = with_ones(values[far, 256:768])
    for r in (1, 0):
        keep(parts.at[r, 3], *join(*zip(store_block(far, flipped, r))))
    arrived(keys.at[0, pl.ds(0, 256)], kv_rs.at[6])
    arrived(keys.at[0, pl.ds(0, 256)], kv_rs.at[7])
    flipped = with_ones(values[far, 0:256])
    keep(p_send, *joined(1, [prefix_block(far, flipped, 1)]))
    p_swap = swap(p_send, p_recv, 1)
    p_swap.start()
    part, stats = joined(0, [prefix_block(far, flipped, 0)])
    p_swap.wait_recv()
    part, stats = join([stats[1:2], p_recv[129:130]], [jnp.concatenate([part, stats], axis=0), p_recv[...]])

    by_row = jnp.transpose(part)
    for t in range(NZ):
        half = stats[:, (t // 4) * 128 : (t // 4 + 1) * 128]
        turned = half if t % 4 == 0 else pltpu.roll(half, 128 - (t % 4) * ROWS, 1)
        z_send[t, 0:ROWS] = by_row[t * ROWS : (t + 1) * ROWS]
        z_send[t, ROWS : ROWS + 2] = turned[0:2]

    for dz in Z_STEPS[:-1]:
        to = z_to[dz]
        remote(z_send.at[to], z_recv.at[z], z_ss, z_rs, x_to[0] + to, y, c).start()
    z_recv[z] = z_send[z]
    left(q_line.at[pl.ds(0, NZ - 1)], q_ss)
    left(keys.at[pl.ds(0, 3)], kv_ss.at[0])
    left(keys.at[pl.ds(0, 3)], kv_ss.at[1])
    q_swap.wait_send()
    p_swap.wait_send()
    weights_swap.wait()
    pl.semaphore_wait(col_sem, 2)
    arrived(z_recv.at[pl.ds(0, NZ - 1)], z_rs)

    side = jnp.concatenate(
        [z_recv[s, ROWS + 1 : ROWS + 2] for s in range(NZ)]
        + [z_recv[s, ROWS : ROWS + 1] for s in range(NZ)]
        + [jnp.zeros((112, 128), F32)],
        axis=0,
    )
    side = jnp.transpose(side)[0:ROWS]
    top = jnp.maximum(jnp.max(side[:, 0:NZ], axis=1, keepdims=True), own_peak)
    own_factor = jnp.exp(own_peak - top)
    total, weighted = own_factor * own_total, own_factor * own_part
    for s in range(NZ):
        factor = jnp.exp(side[:, s : s + 1] - top)
        total = total + factor * side[:, NZ + s : NZ + s + 1]
        weighted = weighted + factor * z_recv[s, 0:ROWS]
    att[chip] = (weighted / total).astype(BF16)

    for dx, dz in FAR_FIRST:
        block = att.at[chip]
        remote(block, block, a_ss, a_rs, x_to[dx] + z_to[dz], y, c).start()
    left(z_send.at[pl.ds(0, NZ - 1)], z_ss)
    arrived(att.at[pl.ds(0, CHIPS - 1)], a_rs)

    att_f32[...] = att[...].reshape(CHIPS * ROWS, HD).astype(F32)
    for h in range(GROUP):
        flat[:, h * HD : (h + 1) * HD] = att_f32[pl.ds(h, 128, stride=GROUP), :].astype(BF16)
    for to_c in (other, c):
        y_send[to_c] = dot_nt(flat[...], wt[to_c]).reshape(NY, 16, 128)
        for dy in Y_STEPS if to_c is other else Y_STEPS[:-1]:
            to_y = y_to[dy]
            remote(y_send.at[to_c, to_y], y_recv.at[yc], y_ss, y_rs, chip, to_y, to_c).start()
    y_recv[yc] = y_send[c, y]
    left(att.at[pl.ds(0, CHIPS - 1)], a_ss)
    arrived(y_recv.at[pl.ds(0, 15)], y_rs)
    for b in range(2):
        summed = functools.reduce(jnp.add, [y_recv[n * 2 + b] for n in range(NY)])
        for n in range(4):
            for i in range(2):
                out_ref[n * 4 + b * 2 + i] = summed[n * 4 + i * 2 : n * 4 + i * 2 + 2, 0:80]

    left(y_recv.at[pl.ds(0, 15)], y_ss)


def body(
    queries,
    new_keys,
    new_values,
    prefix_keys,
    prefix_values,
    prompt_keys,
    prompt_values,
    cache_keys,
    cache_values,
    group_prompt,
    prompt_len,
    cont_prompt,
    cont_len,
    out_weight,
):
    anywhere = pl.BlockSpec(memory_space=pl.ANY)
    vmem = pl.BlockSpec(memory_space=pltpu.VMEM)
    dma = pltpu.SemaphoreType.DMA
    return pl.pallas_call(
        kernel,
        out_shape=jax.ShapeDtypeStruct((16, 2, 80), F32),
        in_specs=[anywhere] * 8 + [vmem] * 3 + [anywhere] * 3,
        out_specs=vmem,
        scratch_shapes=[
            pltpu.SMEM((16,), jnp.int32),
            pltpu.SMEM((16,), jnp.int32),
            pltpu.SMEM((2,), jnp.int32),
            pltpu.VMEM((NZ, ROWS, HD), BF16),
            pltpu.VMEM((NZ, ROWS, HD), BF16),
            pltpu.VMEM((NX, 768, HD), BF16),
            pltpu.VMEM((NX, 768, HD), BF16),
            pltpu.VMEM((2, 256, HD), BF16),
            pltpu.VMEM((2, 256, HD), BF16),
            pltpu.VMEM((2, 128, 1024), BF16),
            pltpu.VMEM((2, 4, 136, 256), F32),
            pltpu.VMEM((136, 256), F32),
            pltpu.VMEM((136, 256), F32),
            pltpu.VMEM((NZ, 34, 128), F32),
            pltpu.VMEM((NZ, 34, 128), F32),
            pltpu.VMEM((CHIPS, ROWS, HD), BF16),
            pltpu.VMEM((CHIPS * ROWS, HD), F32),
            pltpu.VMEM((128, 1024), BF16),
            pltpu.VMEM((2, NY, 16, 128), F32),
            pltpu.VMEM((16, 16, 128), F32),
            dma((11,)),
            dma,
            dma,
            dma((2,)),
            dma((8,)),
            dma((2,)),
            dma((2,)),
            pltpu.SemaphoreType.REGULAR,
            dma,
            dma((2,)),
            dma,
            dma,
            dma,
            dma,
            dma,
            dma,
        ],
        compiler_params=pltpu.CompilerParams(
            collective_id=0, has_side_effects=True, vmem_limit_bytes=55168 << 10
        ),
    )(
        queries.reshape(ROWS, HD),
        prefix_keys[:, 0, :],
        prefix_values[:, 0, :],
        prompt_keys[:, 0, :],
        prompt_values[:, 0, :],
        cache_keys[:, :, 0, :],
        cache_values[:, :, 0, :],
        out_weight.T,
        new_keys[:, :, 0, :],
        new_values[:, :, 0, :],
        cont_prompt.reshape(1, 128),
        group_prompt,
        prompt_len,
        cont_len,
    )


def solution(mesh):
    in_specs = (
        P("seq", None, "kvh", None),
        P("seq", None, "kvh", None),
        P("seq", None, "kvh", None),
        P("seq", "kvh", None),
        P("seq", "kvh", None),
        P("seq", "kvh", None),
        P("seq", "kvh", None),
        P("seq", None, "kvh", None),
        P("seq", None, "kvh", None),
        P(),
        P(),
        P(),
        P("seq"),
        P("kvh", "seq"),
    )
    out_specs = P("kvh", None, "seq")
    return jax.shard_map(body, mesh=mesh, in_specs=in_specs, out_specs=out_specs, check_vma=False)
```

```python
import functools
import math

import jax
import jax.numpy as jnp
from jax import lax
from jax.experimental import pallas as pl
from jax.experimental.pallas import tpu as pltpu
from jax.sharding import PartitionSpec as P

NEG = -1e30
MESH = pl.DeviceIdType.MESH
F32, BF16 = jnp.float32, jnp.bfloat16
NX, NZ, NC, NY = 4, 8, 2, 8
CHIPS = NX * NZ
ROWS = 32
HD = 128
GROUP = 8
SCALING = 1.0 / math.sqrt(HD)


def dot(a, b):
    return jnp.dot(a, b, preferred_element_type=F32)


def dot_nt(a, b):
    return lax.dot_general(a, b, (((1,), (1,)), ((), ())), preferred_element_type=F32)


def iota(shape, axis):
    return lax.broadcasted_iota(jnp.int32, shape, axis)


def loop(low, high, step):
    def run(k, carry):
        step(k)
        return carry

    lax.fori_loop(low, high, run, 0)


def remote(src, dst, send_sem, recv_sem, chip, y, core):
    return pltpu.make_async_remote_copy(
        src_ref=src,
        dst_ref=dst,
        send_sem=send_sem,
        recv_sem=recv_sem,
        device_id={"seq": chip * 2 + core, "kvh": y},
        device_id_type=MESH,
    )


def with_ones(values):
    flipped = jnp.transpose(values.astype(F32))
    return jnp.concatenate([flipped, jnp.ones((16, values.shape[0]), F32)], axis=0).astype(BF16)


X_STEPS, Z_STEPS, Y_STEPS = (2, 1, 3, 0), (4, 3, 5, 2, 6, 1, 7, 0), (4, 3, 5, 2, 6, 1, 7, 0)
FAR_FIRST = [(dx, dz) for dx in X_STEPS for dz in Z_STEPS if dx or dz]


def join(peaks, parts):
    top = functools.reduce(jnp.maximum, peaks)
    total = None
    for peak, part in zip(peaks, parts):
        term = jnp.exp(peak - top) * part
        total = term if total is None else total + term
    stats = jnp.where(iota((8, 256), 0) == 1, top, total[128:136])
    return total[0:128], stats


def kernel(
    q_in,
    pk_in,
    pv_in,
    sk_in,
    sv_in,
    ck_in,
    cv_in,
    w_in,
    nk_ref,
    nv_ref,
    cont_prompt_ref,
    group_prompt_in,
    prompt_len_in,
    cont_len_in,
    out_ref,
    group_prompt_ref,
    prompt_len_ref,
    cont_len_ref,
    q_line,
    q_other,
    keys,
    values,
    ck,
    cv,
    wt,
    parts,
    p_send,
    p_recv,
    z_send,
    z_recv,
    att,
    att_f32,
    flat,
    y_send,
    y_recv,
    own_sem,
    w_ss,
    w_rs,
    kv_ss,
    kv_rs,
    swap_ss,
    swap_rs,
    col_sem,
    q_ss,
    q_rs,
    z_ss,
    z_rs,
    a_ss,
    a_rs,
    y_ss,
    y_rs,
):
    seq = lax.axis_index("seq")
    y = lax.axis_index("kvh")
    chip, c = seq // 2, seq % 2
    x, z = chip // NZ, chip % NZ
    other = 1 - c
    yc = y * 2 + c
    x_at = [lax.rem(x + d, NX) for d in range(NX)]
    x_to = [at * NZ for at in x_at]
    z_to = [lax.rem(z + d, NZ) for d in range(NZ)]
    y_to = [lax.rem(y + d, NY) for d in range(NY)]

    barrier = pltpu.get_barrier_semaphore()

    def greet(to_chip, to_y, to_c, sem=barrier):
        pl.semaphore_signal(
            sem, inc=1, device_id={"seq": to_chip * 2 + to_c, "kvh": to_y}, device_id_type=MESH
        )

    for dx in (1, 3):
        greet(x_to[dx] + z, y, c)
    for dz in (2, 6, 1, 7):
        greet(x_to[0] + z_to[dz], y, c)
    for dy in (1, 7):
        greet(chip, y_to[dy], c)
    greet(chip, y, other)

    local = [
        pltpu.make_async_copy(src, dst, own_sem.at[n])
        for n, (src, dst) in enumerate(
            [
                (q_in, q_line.at[z]),
                (pk_in, keys.at[x, pl.ds(0, 256)]),
                (sk_in, keys.at[x, pl.ds(256, 512)]),
                (pv_in, values.at[x, pl.ds(0, 256)]),
                (sv_in, values.at[x, pl.ds(256, 512)]),
                (ck_in, ck),
                (cv_in, cv),
                (w_in, wt.at[c, pl.ds(0, 80)]),
                (group_prompt_in, group_prompt_ref),
                (prompt_len_in, prompt_len_ref),
                (cont_len_in, cont_len_ref),
            ]
        )
    ]
    pl.semaphore_wait(barrier, 9)

    def arrived(ref, sem):
        remote(ref, ref, q_ss, sem, chip, y, other).wait_recv()

    def left(ref, sem):
        remote(ref, ref, sem, q_rs.at[0], chip, y, other).wait_send()

    def own_to_x(prefix, store, buffer, n, to):
        for src, start, count in ((store, 256, 512), (prefix, 0, 256)):
            dst = buffer.at[x, pl.ds(start, count)]
            remote(src, dst, kv_ss.at[n % 2], kv_rs.at[n], x_to[to] + z, y, c).start()

    def relay(buffer, d, n, to):
        for m, start, count in ((n, 256, 512), (n + 2, 0, 256)):
            block = buffer.at[x_at[d], pl.ds(start, count)]
            remote(block, block, kv_ss.at[n % 2], kv_rs.at[m], x_to[to] + z, y, c).start()

    def swap(src, dst, n):
        return remote(src, dst, swap_ss.at[n], swap_rs.at[n], chip, y, other)

    def q_send(dz, n, to):
        block = q_line.at[z_to[dz]]
        src = block if dz else q_in
        remote(src, block, q_ss, q_rs.at[n], x_to[0] + z_to[to], y, c).start()

    own_to_x(pk_in, sk_in, keys, 0, 1)
    own_to_x(pv_in, sv_in, values, 1, 3)
    for dz in (2, 6, 1, 7):
        q_send(0, 0, dz)
    for copy in local:
        copy.start()
    own_to_x(pv_in, sv_in, values, 3, 1)
    own_to_x(pk_in, sk_in, keys, 2, 3)
    for copy in local:
        copy.wait()
    weights_swap = remote(
        wt.at[c, pl.ds(0, 80)], wt.at[c, pl.ds(0, 80)], w_ss, w_rs, chip, y, other
    )
    weights_swap.start()
    for dy in (1, 7):
        greet(chip, y_to[dy], c, col_sem.at[0])

    wt[:, 80:, :] = jnp.zeros((2, 48, wt.shape[2]), BF16)
    lane = iota((128, 256), 1)
    prompts = jnp.broadcast_to(cont_prompt_ref[...].astype(F32), (8, 128)).astype(BF16)
    prompt_of = []
    for core in (c, other):
        cont = (x * NZ + lane // ROWS) * 4 + core * 2 + (lane % ROWS) // 16
        widen = jnp.where(iota((128, 256), 0) == cont, 1.0, 0.0).astype(BF16)
        prompt_of.append(dot(prompts, widen)[0:1])

    q_own = q_line[z]
    first = iota((ROWS, 1), 0) < 16
    past0 = dot_nt(q_own, ck[0]) * SCALING
    past1 = dot_nt(q_own, ck[1]) * SCALING
    lengths = jnp.where(first, cont_len_ref[0], cont_len_ref[1])
    past = jnp.where(iota(past0.shape, 1) < lengths, jnp.where(first, past0, past1), NEG)
    fresh_pad = jnp.zeros((12, HD), F32)
    nk = jnp.concatenate([nk_ref[0].astype(F32), nk_ref[1].astype(F32), fresh_pad], axis=0).astype(BF16)
    nv = jnp.concatenate([nv_ref[0].astype(F32), nv_ref[1].astype(F32), fresh_pad], axis=0).astype(BF16)
    fresh = dot_nt(q_own, nk) * SCALING
    row, col = iota(fresh.shape, 0), iota(fresh.shape, 1)
    seen = (col // 2 == row // 16) & (col % 2 <= (row // 8) % 2)
    fresh = jnp.where(seen, fresh, NEG)
    own_peak = jnp.maximum(jnp.max(past, axis=1, keepdims=True), jnp.max(fresh, axis=1, keepdims=True))
    past_w = jnp.exp(past - own_peak).astype(BF16)
    fresh_w = jnp.exp(fresh - own_peak).astype(BF16)
    own_total = jnp.sum(past_w.astype(F32), axis=1, keepdims=True) + jnp.sum(
        fresh_w.astype(F32), axis=1, keepdims=True
    )
    own_part = jnp.where(first, dot(past_w, cv[0]), dot(past_w, cv[1])) + dot(fresh_w, nv)
    def rows_of(r):
        return (q_other if r else q_line)[...].reshape(NZ * ROWS, HD)

    def prefix_block(at, flipped, r):
        scores = dot_nt(keys[at, 0:256], rows_of(r)) * SCALING
        peak = jnp.max(scores, axis=0, keepdims=True)
        return peak, dot(flipped, jnp.exp(scores - peak).astype(BF16))[0:136]

    def store_block(at, flipped, r):
        prompt = group_prompt_ref[(at * NZ + z) // 2]
        place = ((z % 2) * 2 + c) * 512 + iota((512, 1), 0)
        scores = dot_nt(keys[at, 256:768], rows_of(r)) * SCALING
        scores = jnp.where(place < prompt_len_ref[prompt], scores, NEG)
        peak = jnp.max(scores, axis=0, keepdims=True)
        part = dot(flipped, jnp.exp(scores - peak).astype(BF16))[0:136]
        mine = prompt_of[r] == jnp.full((1, 256), prompt, jnp.int32).astype(F32)
        return jnp.where(mine, peak, NEG), part

    def keep(ref, part, stats):
        ref[0:128] = part
        ref[128:136] = stats

    def unit(n, at, row_sets):
        flipped = with_ones(values[at])
        for r in row_sets:
            blocks = [prefix_block(at, flipped[:, :256], r), store_block(at, flipped[:, 256:], r)]
            keep(parts.at[r, n], *join(*zip(*blocks)))

    def joined(r, slots, block):
        kept = [(parts[r, n, 129:130], parts[r, n]) for n in slots]
        return join(*zip(*(kept + [block])))

    arrived(q_line.at[pl.ds(0, 4)], q_rs.at[0])
    q_send(1, 1, 6)
    q_send(2, 1, 6)
    q_send(7, 1, 2)
    arrived(keys.at[0], kv_rs.at[0])
    relay(keys, 3, 4, 1)
    arrived(keys.at[0], kv_rs.at[1])
    relay(values, 1, 5, 3)
    arrived(q_line.at[pl.ds(0, 3)], q_rs.at[1])
    q_swap = swap(q_line, q_other, 0)
    q_swap.start()
    unit(0, x, (0,))
    q_swap.wait_recv()
    unit(0, x, (1,))
    pl.semaphore_wait(col_sem.at[0], 2)
    for dy in (2, 6):
        greet(chip, y_to[dy], c, col_sem.at[1])
    arrived(keys.at[0], kv_rs.at[2])
    arrived(keys.at[0], kv_rs.at[3])
    loop(0, 2, lambda i: unit(1 + i, lax.rem(x + 3 - 2 * i, NX), (0, 1)))
    far = x_at[2]
    arrived(keys.at[0, pl.ds(256, 512)], kv_rs.at[4])
    arrived(keys.at[0, pl.ds(256, 512)], kv_rs.at[5])
    flipped = with_ones(values[far, 256:768])
    for r in (1, 0):
        keep(parts.at[r, 3], *joined(r, (0, 1, 2), store_block(far, flipped, r)))
    arrived(keys.at[0, pl.ds(0, 256)], kv_rs.at[6])
    arrived(keys.at[0, pl.ds(0, 256)], kv_rs.at[7])
    flipped = with_ones(values[far, 0:256])
    keep(p_send, *joined(1, (3,), prefix_block(far, flipped, 1)))
    p_swap = swap(p_send, p_recv, 1)
    pl.semaphore_wait(col_sem.at[1], 2)
    p_swap.start()
    part, stats = joined(0, (3,), prefix_block(far, flipped, 0))
    p_swap.wait_recv()
    part, stats = join([stats[1:2], p_recv[129:130]], [jnp.concatenate([part, stats], axis=0), p_recv[...]])

    by_row = jnp.transpose(part)
    for t in range(NZ):
        half = stats[:, (t // 4) * 128 : (t // 4 + 1) * 128]
        turned = half if t % 4 == 0 else pltpu.roll(half, 128 - (t % 4) * ROWS, 1)
        z_send[t, 0:ROWS] = by_row[t * ROWS : (t + 1) * ROWS]
        z_send[t, ROWS : ROWS + 2] = turned[0:2]

    for dz in Z_STEPS[:-1]:
        to = z_to[dz]
        remote(z_send.at[to], z_recv.at[z], z_ss, z_rs, x_to[0] + to, y, c).start()
    z_recv[z] = z_send[z]
    left(q_line.at[pl.ds(0, NZ - 1)], q_ss)
    left(keys.at[pl.ds(0, 3)], kv_ss.at[0])
    left(keys.at[pl.ds(0, 3)], kv_ss.at[1])
    q_swap.wait_send()
    p_swap.wait_send()
    weights_swap.wait()
    arrived(z_recv.at[pl.ds(0, NZ - 1)], z_rs)

    side = jnp.concatenate(
        [z_recv[s, ROWS + 1 : ROWS + 2] for s in range(NZ)]
        + [z_recv[s, ROWS : ROWS + 1] for s in range(NZ)]
        + [jnp.zeros((112, 128), F32)],
        axis=0,
    )
    side = jnp.transpose(side)[0:ROWS]
    top = jnp.maximum(jnp.max(side[:, 0:NZ], axis=1, keepdims=True), own_peak)
    own_factor = jnp.exp(own_peak - top)
    total, weighted = own_factor * own_total, own_factor * own_part
    for s in range(NZ):
        factor = jnp.exp(side[:, s : s + 1] - top)
        total = total + factor * side[:, NZ + s : NZ + s + 1]
        weighted = weighted + factor * z_recv[s, 0:ROWS]
    att[chip] = (weighted / total).astype(BF16)

    def a_copy(dx, to_z):
        block = att.at[chip]
        return remote(block, block, a_ss, a_rs.at[dx], x_to[dx] + to_z, y, c)

    for to_z in range(NZ):
        for dx in X_STEPS[:-1]:
            a_copy(dx, to_z).start()

        @pl.when(to_z != z)
        def _():
            a_copy(0, to_z).start()

    left(z_send.at[pl.ds(0, NZ - 1)], z_ss)
    for d in (0, 1, 3, 2):
        arrived(att.at[pl.ds(0, NZ if d else NZ - 1)], a_rs.at[d])
        at = x_at[(NX - d) % NX]
        att_f32[...] = att[pl.ds(at * NZ, NZ)].reshape(NZ * ROWS, HD).astype(F32)
        for h in range(GROUP):
            tokens = att_f32[pl.ds(h, 32, stride=GROUP), :]
            flat[at, :, h * HD : (h + 1) * HD] = tokens.astype(BF16)
    for to_c in (other, c):
        y_send[to_c] = dot_nt(flat[...].reshape(128, 1024), wt[to_c]).reshape(NY, 16, 128)
        for dy in Y_STEPS if to_c is other else Y_STEPS[:-1]:
            to_y = y_to[dy]
            remote(y_send.at[to_c, to_y], y_recv.at[yc], y_ss, y_rs, chip, to_y, to_c).start()
    y_recv[yc] = y_send[c, y]
    left(att.at[pl.ds(0, CHIPS - 1)], a_ss)
    arrived(y_recv.at[pl.ds(0, 15)], y_rs)
    for b in range(2):
        summed = functools.reduce(jnp.add, [y_recv[n * 2 + b] for n in range(NY)])
        for n in range(4):
            for i in range(2):
                out_ref[n * 4 + b * 2 + i] = summed[n * 4 + i * 2 : n * 4 + i * 2 + 2, 0:80]

    left(y_recv.at[pl.ds(0, 15)], y_ss)


def body(
    queries,
    new_keys,
    new_values,
    prefix_keys,
    prefix_values,
    prompt_keys,
    prompt_values,
    cache_keys,
    cache_values,
    group_prompt,
    prompt_len,
    cont_prompt,
    cont_len,
    out_weight,
):
    anywhere = pl.BlockSpec(memory_space=pl.ANY)
    vmem = pl.BlockSpec(memory_space=pltpu.VMEM)
    dma = pltpu.SemaphoreType.DMA
    return pl.pallas_call(
        kernel,
        out_shape=jax.ShapeDtypeStruct((16, 2, 80), F32),
        in_specs=[anywhere] * 8 + [vmem] * 3 + [anywhere] * 3,
        out_specs=vmem,
        scratch_shapes=[
            pltpu.SMEM((16,), jnp.int32),
            pltpu.SMEM((16,), jnp.int32),
            pltpu.SMEM((2,), jnp.int32),
            pltpu.VMEM((NZ, ROWS, HD), BF16),
            pltpu.VMEM((NZ, ROWS, HD), BF16),
            pltpu.VMEM((NX, 768, HD), BF16),
            pltpu.VMEM((NX, 768, HD), BF16),
            pltpu.VMEM((2, 256, HD), BF16),
            pltpu.VMEM((2, 256, HD), BF16),
            pltpu.VMEM((2, 128, 1024), BF16),
            pltpu.VMEM((2, 4, 136, 256), F32),
            pltpu.VMEM((136, 256), F32),
            pltpu.VMEM((136, 256), F32),
            pltpu.VMEM((NZ, 34, 128), F32),
            pltpu.VMEM((NZ, 34, 128), F32),
            pltpu.VMEM((CHIPS, ROWS, HD), BF16),
            pltpu.VMEM((NZ * ROWS, HD), F32),
            pltpu.VMEM((NX, 32, 1024), BF16),
            pltpu.VMEM((2, NY, 16, 128), F32),
            pltpu.VMEM((16, 16, 128), F32),
            dma((11,)),
            dma,
            dma,
            dma((2,)),
            dma((8,)),
            dma((2,)),
            dma((2,)),
            pltpu.SemaphoreType.REGULAR((2,)),
            dma,
            dma((2,)),
            dma,
            dma,
            dma,
            dma((NX,)),
            dma,
            dma,
        ],
        compiler_params=pltpu.CompilerParams(
            collective_id=0, has_side_effects=True, vmem_limit_bytes=55168 << 10
        ),
    )(
        queries.reshape(ROWS, HD),
        prefix_keys[:, 0, :],
        prefix_values[:, 0, :],
        prompt_keys[:, 0, :],
        prompt_values[:, 0, :],
        cache_keys[:, :, 0, :],
        cache_values[:, :, 0, :],
        out_weight.T,
        new_keys[:, :, 0, :],
        new_values[:, :, 0, :],
        cont_prompt.reshape(1, 128),
        group_prompt,
        prompt_len,
        cont_len,
    )


def solution(mesh):
    in_specs = (
        P("seq", None, "kvh", None),
        P("seq", None, "kvh", None),
        P("seq", None, "kvh", None),
        P("seq", "kvh", None),
        P("seq", "kvh", None),
        P("seq", "kvh", None),
        P("seq", "kvh", None),
        P("seq", None, "kvh", None),
        P("seq", None, "kvh", None),
        P(),
        P(),
        P(),
        P("seq"),
        P("kvh", "seq"),
    )
    out_specs = P("kvh", None, "seq")
    return jax.shard_map(body, mesh=mesh, in_specs=in_specs, out_specs=out_specs, check_vma=False)
```

```python
import functools
import math

import jax
import jax.numpy as jnp
from jax import lax
from jax.experimental import pallas as pl
from jax.experimental.pallas import tpu as pltpu
from jax.sharding import PartitionSpec as P

NEG = -1e30
MESH = pl.DeviceIdType.MESH
F32, BF16 = jnp.float32, jnp.bfloat16
NX, NZ, NC, NY = 4, 8, 2, 8
CHIPS = NX * NZ
ROWS = 32
HD = 128
GROUP = 8
SCALING = 1.0 / math.sqrt(HD)


def dot(a, b):
    return jnp.dot(a, b, preferred_element_type=F32)


def dot_nt(a, b):
    return lax.dot_general(a, b, (((1,), (1,)), ((), ())), preferred_element_type=F32)


def iota(shape, axis):
    return lax.broadcasted_iota(jnp.int32, shape, axis)


def loop(low, high, step):
    def run(k, carry):
        step(k)
        return carry

    lax.fori_loop(low, high, run, 0)


def remote(src, dst, send_sem, recv_sem, chip, y, core):
    return pltpu.make_async_remote_copy(
        src_ref=src,
        dst_ref=dst,
        send_sem=send_sem,
        recv_sem=recv_sem,
        device_id={"seq": chip * 2 + core, "kvh": y},
        device_id_type=MESH,
    )


def with_ones(values):
    flipped = jnp.transpose(values.astype(F32))
    return jnp.concatenate([flipped, jnp.ones((16, values.shape[0]), F32)], axis=0).astype(BF16)


X_STEPS, Z_STEPS, Y_STEPS = (2, 1, 3, 0), (4, 3, 5, 2, 6, 1, 7, 0), (4, 3, 5, 2, 6, 1, 7, 0)
FAR_FIRST = [(dx, dz) for dx in X_STEPS for dz in Z_STEPS if dx or dz]


def join(peaks, parts):
    top = functools.reduce(jnp.maximum, peaks)
    total = None
    for peak, part in zip(peaks, parts):
        term = jnp.exp(peak - top) * part
        total = term if total is None else total + term
    stats = jnp.where(iota((8, 256), 0) == 1, top, total[128:136])
    return total[0:128], stats


def kernel(
    q_in,
    pk_in,
    pv_in,
    sk_in,
    sv_in,
    ck_in,
    cv_in,
    w_in,
    nk_ref,
    nv_ref,
    cont_prompt_ref,
    group_prompt_in,
    prompt_len_in,
    cont_len_in,
    out_ref,
    group_prompt_ref,
    prompt_len_ref,
    cont_len_ref,
    q_line,
    q_other,
    keys,
    values,
    ck,
    cv,
    wt,
    parts,
    p_send,
    p_recv,
    z_send,
    z_recv,
    att,
    att_f32,
    flat,
    y_send,
    y_recv,
    own_sem,
    w_ss,
    w_rs,
    kv_ss,
    kv_rs,
    swap_ss,
    swap_rs,
    col_sem,
    q_ss,
    q_rs,
    z_ss,
    z_rs,
    a_ss,
    a_rs,
    y_ss,
    y_rs,
):
    seq = lax.axis_index("seq")
    y = lax.axis_index("kvh")
    chip, c = seq // 2, seq % 2
    x, z = chip // NZ, chip % NZ
    other = 1 - c
    yc = y * 2 + c
    x_at = [lax.rem(x + d, NX) for d in range(NX)]
    x_to = [at * NZ for at in x_at]
    z_to = [lax.rem(z + d, NZ) for d in range(NZ)]
    y_to = [lax.rem(y + d, NY) for d in range(NY)]

    barrier = pltpu.get_barrier_semaphore()

    def greet(to_chip, to_y, to_c, sem=barrier):
        pl.semaphore_signal(
            sem, inc=1, device_id={"seq": to_chip * 2 + to_c, "kvh": to_y}, device_id_type=MESH
        )

    for dx in (1, 3):
        greet(x_to[dx] + z, y, c)
    for dz in (2, 6, 1, 7):
        greet(x_to[0] + z_to[dz], y, c)
    for dy in (1, 7):
        greet(chip, y_to[dy], c)
    greet(chip, y, other)

    local = [
        pltpu.make_async_copy(src, dst, own_sem.at[n])
        for n, (src, dst) in enumerate(
            [
                (q_in, q_line.at[z]),
                (pk_in, keys.at[x, pl.ds(0, 256)]),
                (sk_in, keys.at[x, pl.ds(256, 512)]),
                (pv_in, values.at[x, pl.ds(0, 256)]),
                (sv_in, values.at[x, pl.ds(256, 512)]),
                (ck_in, ck),
                (cv_in, cv),
                (w_in, wt.at[c, pl.ds(0, 80)]),
                (group_prompt_in, group_prompt_ref),
                (prompt_len_in, prompt_len_ref),
                (cont_len_in, cont_len_ref),
            ]
        )
    ]
    pl.semaphore_wait(barrier, 9)

    def arrived(ref, sem):
        remote(ref, ref, q_ss, sem, chip, y, other).wait_recv()

    def left(ref, sem):
        remote(ref, ref, sem, q_rs.at[0], chip, y, other).wait_send()

    def own_to_x(prefix, store, buffer, n, to):
        for src, start, count in ((store, 256, 512), (prefix, 0, 256)):
            dst = buffer.at[x, pl.ds(start, count)]
            remote(src, dst, kv_ss.at[n % 2], kv_rs.at[n], x_to[to] + z, y, c).start()

    def relay(buffer, d, n, to):
        for m, start, count in ((n, 256, 512), (n + 2, 0, 256)):
            block = buffer.at[x_at[d], pl.ds(start, count)]
            remote(block, block, kv_ss.at[n % 2], kv_rs.at[m], x_to[to] + z, y, c).start()

    def swap(src, dst, n):
        return remote(src, dst, swap_ss.at[n], swap_rs.at[n], chip, y, other)

    def q_send(dz, n, to):
        block = q_line.at[z_to[dz]]
        src = block if dz else q_in
        remote(src, block, q_ss, q_rs.at[n], x_to[0] + z_to[to], y, c).start()

    own_to_x(pk_in, sk_in, keys, 0, 1)
    own_to_x(pv_in, sv_in, values, 1, 3)
    for dz in (2, 6, 1, 7):
        q_send(0, 0, dz)
    for copy in local:
        copy.start()
    own_to_x(pv_in, sv_in, values, 3, 1)
    own_to_x(pk_in, sk_in, keys, 2, 3)
    for copy in local:
        copy.wait()
    weights_swap = remote(
        wt.at[c, pl.ds(0, 80)], wt.at[c, pl.ds(0, 80)], w_ss, w_rs, chip, y, other
    )
    weights_swap.start()
    for dy in (1, 7):
        greet(chip, y_to[dy], c, col_sem.at[0])

    wt[:, 80:, :] = jnp.zeros((2, 48, wt.shape[2]), BF16)
    lane = iota((128, 256), 1)
    prompts = jnp.broadcast_to(cont_prompt_ref[...].astype(F32), (8, 128)).astype(BF16)
    prompt_of = []
    for core in (c, other):
        cont = (x * NZ + lane // ROWS) * 4 + core * 2 + (lane % ROWS) // 16
        widen = jnp.where(iota((128, 256), 0) == cont, 1.0, 0.0).astype(BF16)
        prompt_of.append(dot(prompts, widen)[0:1])

    q_own = q_line[z]
    first = iota((ROWS, 1), 0) < 16
    past0 = dot_nt(q_own, ck[0]) * SCALING
    past1 = dot_nt(q_own, ck[1]) * SCALING
    lengths = jnp.where(first, cont_len_ref[0], cont_len_ref[1])
    past = jnp.where(iota(past0.shape, 1) < lengths, jnp.where(first, past0, past1), NEG)
    fresh_pad = jnp.zeros((12, HD), F32)
    nk = jnp.concatenate([nk_ref[0].astype(F32), nk_ref[1].astype(F32), fresh_pad], axis=0).astype(BF16)
    nv = jnp.concatenate([nv_ref[0].astype(F32), nv_ref[1].astype(F32), fresh_pad], axis=0).astype(BF16)
    fresh = dot_nt(q_own, nk) * SCALING
    row, col = iota(fresh.shape, 0), iota(fresh.shape, 1)
    seen = (col // 2 == row // 16) & (col % 2 <= (row // 8) % 2)
    fresh = jnp.where(seen, fresh, NEG)
    own_peak = jnp.maximum(jnp.max(past, axis=1, keepdims=True), jnp.max(fresh, axis=1, keepdims=True))
    past_w = jnp.exp(past - own_peak).astype(BF16)
    fresh_w = jnp.exp(fresh - own_peak).astype(BF16)
    own_total = jnp.sum(past_w.astype(F32), axis=1, keepdims=True) + jnp.sum(
        fresh_w.astype(F32), axis=1, keepdims=True
    )
    own_part = jnp.where(first, dot(past_w, cv[0]), dot(past_w, cv[1])) + dot(fresh_w, nv)
    def rows_of(r):
        return (q_other if r else q_line)[...].reshape(NZ * ROWS, HD)

    def prefix_block(at, flipped, r):
        scores = dot_nt(keys[at, 0:256], rows_of(r)) * SCALING
        peak = jnp.max(scores, axis=0, keepdims=True)
        return peak, dot(flipped, jnp.exp(scores - peak).astype(BF16))[0:136]

    def store_block(at, flipped, r):
        prompt = group_prompt_ref[(at * NZ + z) // 2]
        place = ((z % 2) * 2 + c) * 512 + iota((512, 1), 0)
        scores = dot_nt(keys[at, 256:768], rows_of(r)) * SCALING
        scores = jnp.where(place < prompt_len_ref[prompt], scores, NEG)
        peak = jnp.max(scores, axis=0, keepdims=True)
        part = dot(flipped, jnp.exp(scores - peak).astype(BF16))[0:136]
        mine = prompt_of[r] == jnp.full((1, 256), prompt, jnp.int32).astype(F32)
        return jnp.where(mine, peak, NEG), part

    def keep(ref, part, stats):
        ref[0:128] = part
        ref[128:136] = stats

    def unit(n, at, row_sets):
        flipped = with_ones(values[at])
        for r in row_sets:
            blocks = [prefix_block(at, flipped[:, :256], r), store_block(at, flipped[:, 256:], r)]
            keep(parts.at[r, n], *join(*zip(*blocks)))

    def joined(r, slots, block):
        kept = [(parts[r, n, 129:130], parts[r, n]) for n in slots]
        return join(*zip(*(kept + [block])))

    arrived(q_line.at[pl.ds(0, 4)], q_rs.at[0])
    q_send(1, 1, 6)
    q_send(2, 1, 6)
    q_send(7, 1, 2)
    arrived(keys.at[0], kv_rs.at[0])
    relay(keys, 3, 4, 1)
    arrived(keys.at[0], kv_rs.at[1])
    relay(values, 1, 5, 3)
    arrived(q_line.at[pl.ds(0, 3)], q_rs.at[1])
    q_swap = swap(q_line, q_other, 0)
    q_swap.start()
    unit(0, x, (0,))
    q_swap.wait_recv()
    unit(0, x, (1,))
    pl.semaphore_wait(col_sem.at[0], 2)
    for dy in (2, 6):
        greet(chip, y_to[dy], c, col_sem.at[1])
    arrived(keys.at[0], kv_rs.at[2])
    arrived(keys.at[0], kv_rs.at[3])
    loop(0, 2, lambda i: unit(1 + i, lax.rem(x + 3 - 2 * i, NX), (0, 1)))
    far = x_at[2]
    arrived(keys.at[0, pl.ds(256, 512)], kv_rs.at[4])
    arrived(keys.at[0, pl.ds(256, 512)], kv_rs.at[5])
    flipped = with_ones(values[far, 256:768])
    for r in (1, 0):
        keep(parts.at[r, 3], *joined(r, (0, 1, 2), store_block(far, flipped, r)))
    arrived(keys.at[0, pl.ds(0, 256)], kv_rs.at[6])
    arrived(keys.at[0, pl.ds(0, 256)], kv_rs.at[7])
    flipped = with_ones(values[far, 0:256])
    keep(p_send, *joined(1, (3,), prefix_block(far, flipped, 1)))
    p_swap = swap(p_send, p_recv, 1)
    pl.semaphore_wait(col_sem.at[1], 2)
    p_swap.start()
    part, stats = joined(0, (3,), prefix_block(far, flipped, 0))
    p_swap.wait_recv()
    part, stats = join([stats[1:2], p_recv[129:130]], [jnp.concatenate([part, stats], axis=0), p_recv[...]])

    by_row = jnp.transpose(part)
    for t in range(NZ):
        half = stats[:, (t // 4) * 128 : (t // 4 + 1) * 128]
        turned = half if t % 4 == 0 else pltpu.roll(half, 128 - (t % 4) * ROWS, 1)
        z_send[t, 0:ROWS] = by_row[t * ROWS : (t + 1) * ROWS]
        z_send[t, ROWS : ROWS + 2] = turned[0:2]

    for dz in Z_STEPS[:-1]:
        to = z_to[dz]
        remote(z_send.at[to], z_recv.at[z], z_ss, z_rs, x_to[0] + to, y, c).start()
    z_recv[z] = z_send[z]
    left(q_line.at[pl.ds(0, NZ - 1)], q_ss)
    left(keys.at[pl.ds(0, 3)], kv_ss.at[0])
    left(keys.at[pl.ds(0, 3)], kv_ss.at[1])
    q_swap.wait_send()
    p_swap.wait_send()
    weights_swap.wait()
    arrived(z_recv.at[pl.ds(0, NZ - 1)], z_rs)

    side = jnp.concatenate(
        [z_recv[s, ROWS + 1 : ROWS + 2] for s in range(NZ)]
        + [z_recv[s, ROWS : ROWS + 1] for s in range(NZ)]
        + [jnp.zeros((112, 128), F32)],
        axis=0,
    )
    side = jnp.transpose(side)[0:ROWS]
    top = jnp.maximum(jnp.max(side[:, 0:NZ], axis=1, keepdims=True), own_peak)
    own_factor = jnp.exp(own_peak - top)
    total, weighted = own_factor * own_total, own_factor * own_part
    for s in range(NZ):
        factor = jnp.exp(side[:, s : s + 1] - top)
        total = total + factor * side[:, NZ + s : NZ + s + 1]
        weighted = weighted + factor * z_recv[s, 0:ROWS]
    att[chip] = (weighted / total).astype(BF16)

    def a_copy(dx, to_z):
        block = att.at[chip]
        return remote(block, block, a_ss, a_rs.at[dx], x_to[dx] + to_z, y, c)

    for to_z in range(NZ):
        for dx in X_STEPS[:-1]:
            a_copy(dx, to_z).start()

        @pl.when(to_z != z)
        def _():
            a_copy(0, to_z).start()

    left(z_send.at[pl.ds(0, NZ - 1)], z_ss)

    def project(at):
        for to_c in (other, c):
            y_send[to_c, pl.ds(at * 2, 2)] = dot_nt(flat[at], wt[to_c]).reshape(2, 16, 128)
        for to_y in (at * 2, at * 2 + 1):
            y_copy(to_y, other).start()

            @pl.when(to_y != y)
            def _():
                y_copy(to_y, c).start()

            @pl.when(to_y == y)
            def _():
                y_recv[yc] = y_send[c, to_y]

    def y_copy(to_y, to_c):
        return remote(y_send.at[to_c, to_y], y_recv.at[yc], y_ss, y_rs, chip, to_y, to_c)

    for d in (0, 1, 3, 2):
        arrived(att.at[pl.ds(0, NZ if d else NZ - 1)], a_rs.at[d])
        at = x_at[(NX - d) % NX]
        att_f32[...] = att[pl.ds(at * NZ, NZ)].reshape(NZ * ROWS, HD).astype(F32)
        for h in range(GROUP):
            tokens = att_f32[pl.ds(h, 32, stride=GROUP), :]
            flat[at, :, h * HD : (h + 1) * HD] = tokens.astype(BF16)
        project(at)
    left(att.at[pl.ds(0, CHIPS - 1)], a_ss)
    arrived(y_recv.at[pl.ds(0, 15)], y_rs)
    for b in range(2):
        summed = functools.reduce(jnp.add, [y_recv[n * 2 + b] for n in range(NY)])
        for n in range(4):
            for i in range(2):
                out_ref[n * 4 + b * 2 + i] = summed[n * 4 + i * 2 : n * 4 + i * 2 + 2, 0:80]

    left(y_recv.at[pl.ds(0, 15)], y_ss)


def body(
    queries,
    new_keys,
    new_values,
    prefix_keys,
    prefix_values,
    prompt_keys,
    prompt_values,
    cache_keys,
    cache_values,
    group_prompt,
    prompt_len,
    cont_prompt,
    cont_len,
    out_weight,
):
    anywhere = pl.BlockSpec(memory_space=pl.ANY)
    vmem = pl.BlockSpec(memory_space=pltpu.VMEM)
    dma = pltpu.SemaphoreType.DMA
    return pl.pallas_call(
        kernel,
        out_shape=jax.ShapeDtypeStruct((16, 2, 80), F32),
        in_specs=[anywhere] * 8 + [vmem] * 3 + [anywhere] * 3,
        out_specs=vmem,
        scratch_shapes=[
            pltpu.SMEM((16,), jnp.int32),
            pltpu.SMEM((16,), jnp.int32),
            pltpu.SMEM((2,), jnp.int32),
            pltpu.VMEM((NZ, ROWS, HD), BF16),
            pltpu.VMEM((NZ, ROWS, HD), BF16),
            pltpu.VMEM((NX, 768, HD), BF16),
            pltpu.VMEM((NX, 768, HD), BF16),
            pltpu.VMEM((2, 256, HD), BF16),
            pltpu.VMEM((2, 256, HD), BF16),
            pltpu.VMEM((2, 128, 1024), BF16),
            pltpu.VMEM((2, 4, 136, 256), F32),
            pltpu.VMEM((136, 256), F32),
            pltpu.VMEM((136, 256), F32),
            pltpu.VMEM((NZ, 34, 128), F32),
            pltpu.VMEM((NZ, 34, 128), F32),
            pltpu.VMEM((CHIPS, ROWS, HD), BF16),
            pltpu.VMEM((NZ * ROWS, HD), F32),
            pltpu.VMEM((NX, 32, 1024), BF16),
            pltpu.VMEM((2, NY, 16, 128), F32),
            pltpu.VMEM((16, 16, 128), F32),
            dma((11,)),
            dma,
            dma,
            dma((2,)),
            dma((8,)),
            dma((2,)),
            dma((2,)),
            pltpu.SemaphoreType.REGULAR((2,)),
            dma,
            dma((2,)),
            dma,
            dma,
            dma,
            dma((NX,)),
            dma,
            dma,
        ],
        compiler_params=pltpu.CompilerParams(
            collective_id=0, has_side_effects=True, vmem_limit_bytes=55168 << 10
        ),
    )(
        queries.reshape(ROWS, HD),
        prefix_keys[:, 0, :],
        prefix_values[:, 0, :],
        prompt_keys[:, 0, :],
        prompt_values[:, 0, :],
        cache_keys[:, :, 0, :],
        cache_values[:, :, 0, :],
        out_weight.T,
        new_keys[:, :, 0, :],
        new_values[:, :, 0, :],
        cont_prompt.reshape(1, 128),
        group_prompt,
        prompt_len,
        cont_len,
    )


def solution(mesh):
    in_specs = (
        P("seq", None, "kvh", None),
        P("seq", None, "kvh", None),
        P("seq", None, "kvh", None),
        P("seq", "kvh", None),
        P("seq", "kvh", None),
        P("seq", "kvh", None),
        P("seq", "kvh", None),
        P("seq", None, "kvh", None),
        P("seq", None, "kvh", None),
        P(),
        P(),
        P(),
        P("seq"),
        P("kvh", "seq"),
    )
    out_specs = P("kvh", None, "seq")
    return jax.shard_map(body, mesh=mesh, in_specs=in_specs, out_specs=out_specs, check_vma=False)
```

```python
import functools
import math

import jax
import jax.numpy as jnp
from jax import lax
from jax.experimental import pallas as pl
from jax.experimental.pallas import tpu as pltpu
from jax.sharding import PartitionSpec as P

NEG = -1e30
MESH = pl.DeviceIdType.MESH
F32, BF16 = jnp.float32, jnp.bfloat16
NX, NZ, NC, NY = 4, 8, 2, 8
CHIPS = NX * NZ
ROWS = 32
HD = 128
GROUP = 8
SCALING = 1.0 / math.sqrt(HD)


def dot(a, b):
    return jnp.dot(a, b, preferred_element_type=F32)


def dot_nt(a, b):
    return lax.dot_general(a, b, (((1,), (1,)), ((), ())), preferred_element_type=F32)


def iota(shape, axis):
    return lax.broadcasted_iota(jnp.int32, shape, axis)


def loop(low, high, step):
    def run(k, carry):
        step(k)
        return carry

    lax.fori_loop(low, high, run, 0)


def remote(src, dst, send_sem, recv_sem, chip, y, core):
    return pltpu.make_async_remote_copy(
        src_ref=src,
        dst_ref=dst,
        send_sem=send_sem,
        recv_sem=recv_sem,
        device_id={"seq": chip * 2 + core, "kvh": y},
        device_id_type=MESH,
    )


def with_ones(values):
    flipped = jnp.transpose(values.astype(F32))
    return jnp.concatenate([flipped, jnp.ones((16, values.shape[0]), F32)], axis=0).astype(BF16)


X_STEPS, Z_STEPS, Y_STEPS = (2, 1, 3, 0), (4, 3, 5, 2, 6, 1, 7, 0), (4, 3, 5, 2, 6, 1, 7, 0)
FAR_FIRST = [(dx, dz) for dx in X_STEPS for dz in Z_STEPS if dx or dz]


def join(peaks, parts):
    top = functools.reduce(jnp.maximum, peaks)
    total = None
    for peak, part in zip(peaks, parts):
        term = jnp.exp(peak - top) * part
        total = term if total is None else total + term
    stats = jnp.where(iota((8, 256), 0) == 1, top, total[128:136])
    return total[0:128], stats


def kernel(
    q_in,
    pk_in,
    pv_in,
    sk_in,
    sv_in,
    ck_in,
    cv_in,
    w_in,
    nk_ref,
    nv_ref,
    cont_prompt_ref,
    group_prompt_in,
    prompt_len_in,
    cont_len_in,
    out_ref,
    group_prompt_ref,
    prompt_len_ref,
    cont_len_ref,
    q_line,
    q_other,
    keys,
    values,
    ck,
    cv,
    wt,
    parts,
    p_send,
    p_recv,
    z_send,
    z_recv,
    att,
    att_f32,
    flat,
    y_send,
    y_recv,
    own_sem,
    w_ss,
    w_rs,
    kv_ss,
    kv_rs,
    swap_ss,
    swap_rs,
    col_sem,
    q_ss,
    q_rs,
    z_ss,
    z_rs,
    a_ss,
    a_rs,
    y_ss,
    y_rs,
):
    seq = lax.axis_index("seq")
    y = lax.axis_index("kvh")
    chip, c = seq // 2, seq % 2
    x, z = chip // NZ, chip % NZ
    other = 1 - c
    yc = y * 2 + c
    x_at = [lax.rem(x + d, NX) for d in range(NX)]
    x_to = [at * NZ for at in x_at]
    z_to = [lax.rem(z + d, NZ) for d in range(NZ)]
    y_to = [lax.rem(y + d, NY) for d in range(NY)]

    barrier = pltpu.get_barrier_semaphore()

    def greet(to_chip, to_y, to_c, sem=barrier):
        pl.semaphore_signal(
            sem, inc=1, device_id={"seq": to_chip * 2 + to_c, "kvh": to_y}, device_id_type=MESH
        )

    for dx in (1, 3):
        greet(x_to[dx] + z, y, c)
    for dz in (2, 6, 1, 7):
        greet(x_to[0] + z_to[dz], y, c)
    for dy in (1, 7):
        greet(chip, y_to[dy], c)
    greet(chip, y, other)

    local = [
        pltpu.make_async_copy(src, dst, own_sem.at[n])
        for n, (src, dst) in enumerate(
            [
                (q_in, q_line.at[z]),
                (pk_in, keys.at[x, pl.ds(0, 256)]),
                (sk_in, keys.at[x, pl.ds(256, 512)]),
                (pv_in, values.at[x, pl.ds(0, 256)]),
                (sv_in, values.at[x, pl.ds(256, 512)]),
                (ck_in, ck),
                (cv_in, cv),
                (w_in, wt.at[c, pl.ds(0, 80)]),
                (group_prompt_in, group_prompt_ref),
                (prompt_len_in, prompt_len_ref),
                (cont_len_in, cont_len_ref),
            ]
        )
    ]
    pl.semaphore_wait(barrier, 9)

    def arrived(ref, sem):
        remote(ref, ref, q_ss, sem, chip, y, other).wait_recv()

    def left(ref, sem):
        remote(ref, ref, sem, q_rs.at[0], chip, y, other).wait_send()

    def own_to_x(prefix, store, buffer, n, to):
        for src, start, count in ((store, 256, 512), (prefix, 0, 256)):
            dst = buffer.at[x, pl.ds(start, count)]
            remote(src, dst, kv_ss.at[n % 2], kv_rs.at[n], x_to[to] + z, y, c).start()

    def relay(buffer, d, n, to):
        for m, start, count in ((n, 256, 512), (n + 2, 0, 256)):
            block = buffer.at[x_at[d], pl.ds(start, count)]
            remote(block, block, kv_ss.at[n % 2], kv_rs.at[m], x_to[to] + z, y, c).start()

    def swap(src, dst, n):
        return remote(src, dst, swap_ss.at[n], swap_rs.at[n], chip, y, other)

    def q_send(dz, n, to):
        block = q_line.at[z_to[dz]]
        src = block if dz else q_in
        remote(src, block, q_ss, q_rs.at[n], x_to[0] + z_to[to], y, c).start()

    own_to_x(pk_in, sk_in, keys, 0, 1)
    own_to_x(pv_in, sv_in, values, 1, 3)
    for dz in (2, 6, 1, 7):
        q_send(0, 0, dz)
    for copy in local:
        copy.start()
    own_to_x(pv_in, sv_in, values, 3, 1)
    own_to_x(pk_in, sk_in, keys, 2, 3)
    for copy in local:
        copy.wait()
    weights_swap = remote(
        wt.at[c, pl.ds(0, 80)], wt.at[c, pl.ds(0, 80)], w_ss, w_rs, chip, y, other
    )
    weights_swap.start()
    for dy in (1, 7):
        greet(chip, y_to[dy], c, col_sem.at[0])

    wt[:, 80:, :] = jnp.zeros((2, 48, wt.shape[2]), BF16)
    lane = iota((128, 256), 1)
    prompts = jnp.broadcast_to(cont_prompt_ref[...].astype(F32), (8, 128)).astype(BF16)
    prompt_of = []
    for core in (c, other):
        cont = (x * NZ + lane // ROWS) * 4 + core * 2 + (lane % ROWS) // 16
        widen = jnp.where(iota((128, 256), 0) == cont, 1.0, 0.0).astype(BF16)
        prompt_of.append(dot(prompts, widen)[0:1])

    q_own = q_line[z]
    first = iota((ROWS, 1), 0) < 16
    past0 = dot_nt(q_own, ck[0]) * SCALING
    past1 = dot_nt(q_own, ck[1]) * SCALING
    lengths = jnp.where(first, cont_len_ref[0], cont_len_ref[1])
    past = jnp.where(iota(past0.shape, 1) < lengths, jnp.where(first, past0, past1), NEG)
    fresh_pad = jnp.zeros((12, HD), F32)
    nk = jnp.concatenate([nk_ref[0].astype(F32), nk_ref[1].astype(F32), fresh_pad], axis=0).astype(BF16)
    nv = jnp.concatenate([nv_ref[0].astype(F32), nv_ref[1].astype(F32), fresh_pad], axis=0).astype(BF16)
    fresh = dot_nt(q_own, nk) * SCALING
    row, col = iota(fresh.shape, 0), iota(fresh.shape, 1)
    seen = (col // 2 == row // 16) & (col % 2 <= (row // 8) % 2)
    fresh = jnp.where(seen, fresh, NEG)
    own_peak = jnp.maximum(jnp.max(past, axis=1, keepdims=True), jnp.max(fresh, axis=1, keepdims=True))
    past_w = jnp.exp(past - own_peak).astype(BF16)
    fresh_w = jnp.exp(fresh - own_peak).astype(BF16)
    own_total = jnp.sum(past_w.astype(F32), axis=1, keepdims=True) + jnp.sum(
        fresh_w.astype(F32), axis=1, keepdims=True
    )
    own_part = jnp.where(first, dot(past_w, cv[0]), dot(past_w, cv[1])) + dot(fresh_w, nv)
    def rows_of(r):
        return (q_other if r else q_line)[...].reshape(NZ * ROWS, HD)

    def prefix_block(at, flipped, r):
        scores = dot_nt(keys[at, 0:256], rows_of(r)) * SCALING
        peak = jnp.max(scores, axis=0, keepdims=True)
        return peak, dot(flipped, jnp.exp(scores - peak).astype(BF16))[0:136]

    def store_block(at, flipped, r):
        prompt = group_prompt_ref[(at * NZ + z) // 2]
        place = ((z % 2) * 2 + c) * 512 + iota((512, 1), 0)
        scores = dot_nt(keys[at, 256:768], rows_of(r)) * SCALING
        scores = jnp.where(place < prompt_len_ref[prompt], scores, NEG)
        peak = jnp.max(scores, axis=0, keepdims=True)
        part = dot(flipped, jnp.exp(scores - peak).astype(BF16))[0:136]
        mine = prompt_of[r] == jnp.full((1, 256), prompt, jnp.int32).astype(F32)
        return jnp.where(mine, peak, NEG), part

    def keep(ref, part, stats):
        ref[0:128] = part
        ref[128:136] = stats

    def unit(n, at, row_sets):
        flipped = with_ones(values[at])
        for r in row_sets:
            blocks = [prefix_block(at, flipped[:, :256], r), store_block(at, flipped[:, 256:], r)]
            keep(parts.at[r, n], *join(*zip(*blocks)))

    def joined(r, slots, block):
        kept = [(parts[r, n, 129:130], parts[r, n]) for n in slots]
        return join(*zip(*(kept + [block])))

    arrived(q_line.at[pl.ds(0, 4)], q_rs.at[0])
    q_send(1, 1, 6)
    q_send(2, 1, 6)
    q_send(7, 1, 2)
    arrived(keys.at[0], kv_rs.at[0])
    relay(keys, 3, 4, 1)
    arrived(keys.at[0], kv_rs.at[1])
    relay(values, 1, 5, 3)
    arrived(q_line.at[pl.ds(0, 3)], q_rs.at[1])
    q_swap = swap(q_line, q_other, 0)
    q_swap.start()
    unit(0, x, (0,))
    q_swap.wait_recv()
    unit(0, x, (1,))
    pl.semaphore_wait(col_sem.at[0], 2)
    for dy in (2, 6):
        greet(chip, y_to[dy], c, col_sem.at[1])
    arrived(keys.at[0], kv_rs.at[2])
    arrived(keys.at[0], kv_rs.at[3])
    loop(0, 2, lambda i: unit(1 + i, lax.rem(x + 3 - 2 * i, NX), (0, 1)))
    far = x_at[2]
    arrived(keys.at[0, pl.ds(256, 512)], kv_rs.at[4])
    arrived(keys.at[0, pl.ds(256, 512)], kv_rs.at[5])
    flipped = with_ones(values[far, 256:768])
    for r in (1, 0):
        keep(parts.at[r, 3], *joined(r, (0, 1, 2), store_block(far, flipped, r)))
    arrived(keys.at[0, pl.ds(0, 256)], kv_rs.at[6])
    arrived(keys.at[0, pl.ds(0, 256)], kv_rs.at[7])
    flipped = with_ones(values[far, 0:256])
    keep(p_send, *joined(1, (3,), prefix_block(far, flipped, 1)))
    p_swap = swap(p_send, p_recv, 1)
    pl.semaphore_wait(col_sem.at[1], 2)
    p_swap.start()
    part, stats = joined(0, (3,), prefix_block(far, flipped, 0))
    p_swap.wait_recv()
    part, stats = join([stats[1:2], p_recv[129:130]], [jnp.concatenate([part, stats], axis=0), p_recv[...]])

    by_row = jnp.transpose(part)
    for t in range(NZ):
        half = stats[:, (t // 4) * 128 : (t // 4 + 1) * 128]
        turned = half if t % 4 == 0 else pltpu.roll(half, 128 - (t % 4) * ROWS, 1)
        z_send[t, 0:ROWS] = by_row[t * ROWS : (t + 1) * ROWS]
        z_send[t, ROWS : ROWS + 2] = turned[0:2]

    for dz in Z_STEPS[:-1]:
        to = z_to[dz]
        remote(z_send.at[to], z_recv.at[z], z_ss, z_rs, x_to[0] + to, y, c).start()
    z_recv[z] = z_send[z]
    left(q_line.at[pl.ds(0, NZ - 1)], q_ss)
    left(keys.at[pl.ds(0, 3)], kv_ss.at[0])
    left(keys.at[pl.ds(0, 3)], kv_ss.at[1])
    q_swap.wait_send()
    p_swap.wait_send()
    weights_swap.wait()
    arrived(z_recv.at[pl.ds(0, NZ - 1)], z_rs)

    side = jnp.concatenate(
        [z_recv[s, ROWS + 1 : ROWS + 2] for s in range(NZ)]
        + [z_recv[s, ROWS : ROWS + 1] for s in range(NZ)]
        + [jnp.zeros((112, 128), F32)],
        axis=0,
    )
    side = jnp.transpose(side)[0:ROWS]
    top = jnp.maximum(jnp.max(side[:, 0:NZ], axis=1, keepdims=True), own_peak)
    own_factor = jnp.exp(own_peak - top)
    total, weighted = own_factor * own_total, own_factor * own_part
    for s in range(NZ):
        factor = jnp.exp(side[:, s : s + 1] - top)
        total = total + factor * side[:, NZ + s : NZ + s + 1]
        weighted = weighted + factor * z_recv[s, 0:ROWS]
    att[chip] = (weighted / total).astype(BF16)

    def a_copy(dx, to_z):
        block = att.at[chip]
        return remote(block, block, a_ss, a_rs.at[dx], x_to[dx] + to_z, y, c)

    for to_z in range(NZ):
        for to_x in (0, 1, 3, 2):
            dx = lax.rem(to_x - x + NX, NX)
            block = att.at[chip]
            copy = remote(block, block, a_ss, a_rs.at[dx], to_x * NZ + to_z, y, c)
            pl.when((to_z != z) | (to_x != x))(copy.start)
    left(z_send.at[pl.ds(0, NZ - 1)], z_ss)

    def project(at):
        for to_c in (other, c):
            y_send[to_c, pl.ds(at * 2, 2)] = dot_nt(flat[at], wt[to_c]).reshape(2, 16, 128)
        for to_y in (at * 2, at * 2 + 1):
            y_copy(to_y, other).start()

            @pl.when(to_y != y)
            def _():
                y_copy(to_y, c).start()

            @pl.when(to_y == y)
            def _():
                y_recv[yc] = y_send[c, to_y]

    def y_copy(to_y, to_c):
        return remote(y_send.at[to_c, to_y], y_recv.at[yc], y_ss, y_rs, chip, to_y, to_c)

    for d in (0, 1, 3, 2):
        arrived(att.at[pl.ds(0, NZ if d else NZ - 1)], a_rs.at[d])
        at = x_at[(NX - d) % NX]
        att_f32[...] = att[pl.ds(at * NZ, NZ)].reshape(NZ * ROWS, HD).astype(F32)
        for h in range(GROUP):
            tokens = att_f32[pl.ds(h, 32, stride=GROUP), :]
            flat[at, :, h * HD : (h + 1) * HD] = tokens.astype(BF16)
        project(at)
    left(att.at[pl.ds(0, CHIPS - 1)], a_ss)
    arrived(y_recv.at[pl.ds(0, 15)], y_rs)
    for b in range(2):
        summed = functools.reduce(jnp.add, [y_recv[n * 2 + b] for n in range(NY)])
        for n in range(4):
            for i in range(2):
                out_ref[n * 4 + b * 2 + i] = summed[n * 4 + i * 2 : n * 4 + i * 2 + 2, 0:80]

    left(y_recv.at[pl.ds(0, 15)], y_ss)


def body(
    queries,
    new_keys,
    new_values,
    prefix_keys,
    prefix_values,
    prompt_keys,
    prompt_values,
    cache_keys,
    cache_values,
    group_prompt,
    prompt_len,
    cont_prompt,
    cont_len,
    out_weight,
):
    anywhere = pl.BlockSpec(memory_space=pl.ANY)
    vmem = pl.BlockSpec(memory_space=pltpu.VMEM)
    dma = pltpu.SemaphoreType.DMA
    return pl.pallas_call(
        kernel,
        out_shape=jax.ShapeDtypeStruct((16, 2, 80), F32),
        in_specs=[anywhere] * 8 + [vmem] * 3 + [anywhere] * 3,
        out_specs=vmem,
        scratch_shapes=[
            pltpu.SMEM((16,), jnp.int32),
            pltpu.SMEM((16,), jnp.int32),
            pltpu.SMEM((2,), jnp.int32),
            pltpu.VMEM((NZ, ROWS, HD), BF16),
            pltpu.VMEM((NZ, ROWS, HD), BF16),
            pltpu.VMEM((NX, 768, HD), BF16),
            pltpu.VMEM((NX, 768, HD), BF16),
            pltpu.VMEM((2, 256, HD), BF16),
            pltpu.VMEM((2, 256, HD), BF16),
            pltpu.VMEM((2, 128, 1024), BF16),
            pltpu.VMEM((2, 4, 136, 256), F32),
            pltpu.VMEM((136, 256), F32),
            pltpu.VMEM((136, 256), F32),
            pltpu.VMEM((NZ, 34, 128), F32),
            pltpu.VMEM((NZ, 34, 128), F32),
            pltpu.VMEM((CHIPS, ROWS, HD), BF16),
            pltpu.VMEM((NZ * ROWS, HD), F32),
            pltpu.VMEM((NX, 32, 1024), BF16),
            pltpu.VMEM((2, NY, 16, 128), F32),
            pltpu.VMEM((16, 16, 128), F32),
            dma((11,)),
            dma,
            dma,
            dma((2,)),
            dma((8,)),
            dma((2,)),
            dma((2,)),
            pltpu.SemaphoreType.REGULAR((2,)),
            dma,
            dma((2,)),
            dma,
            dma,
            dma,
            dma((NX,)),
            dma,
            dma,
        ],
        compiler_params=pltpu.CompilerParams(
            collective_id=0, has_side_effects=True, vmem_limit_bytes=55168 << 10
        ),
    )(
        queries.reshape(ROWS, HD),
        prefix_keys[:, 0, :],
        prefix_values[:, 0, :],
        prompt_keys[:, 0, :],
        prompt_values[:, 0, :],
        cache_keys[:, :, 0, :],
        cache_values[:, :, 0, :],
        out_weight.T,
        new_keys[:, :, 0, :],
        new_values[:, :, 0, :],
        cont_prompt.reshape(1, 128),
        group_prompt,
        prompt_len,
        cont_len,
    )


def solution(mesh):
    in_specs = (
        P("seq", None, "kvh", None),
        P("seq", None, "kvh", None),
        P("seq", None, "kvh", None),
        P("seq", "kvh", None),
        P("seq", "kvh", None),
        P("seq", "kvh", None),
        P("seq", "kvh", None),
        P("seq", None, "kvh", None),
        P("seq", None, "kvh", None),
        P(),
        P(),
        P(),
        P("seq"),
        P("kvh", "seq"),
    )
    out_specs = P("kvh", None, "seq")
    return jax.shard_map(body, mesh=mesh, in_specs=in_specs, out_specs=out_specs, check_vma=False)
```
